128 devices in a mesh: tm: 4 (over x_hi, core), space: 32 (over z, y, x_lo).
Axes of the slice: x: 4 (x_hi: 2, x_lo: 2; x = x_hi * 2 + x_lo), y: 4, z: 4, core: 2. Of those that a mesh axis runs over, the one named last changes fastest.
Arguments:
- inv_local: float32 [4, 2048, 2048], P('tm', 'space'), as said below
- coupling: float32 [4, 2048, 2048], P('tm', 'space')
- tail_block: float32 [2048, 2048], P('space'), as said below
- adjacency: int32 [16, 16], replicated, may hold values 0 or 1
Outputs:
- sel_diag: float32 [4, 2048, 2048], P('tm', 'space')
- sel_off: float32 [4, 2048, 2048], P('tm', 'space')
The draws below stay inside these ranges and needn't reach their ends.
Inputs may be any that keep to these rules, and one draw needn't show every extreme that they name: Every block inv_local[t] is symmetric. tail_block is symmetric.
All inputs are finite; a program needn't handle non-finite values.
Results may differ from the reference program's by a relative error of at most 0.00011.
Values sent between devices are 32-bit elements; how exact they have to be, the bound alone decides.
No kernel may reach another device: no remote copies, remote signals or barrier semaphores. Data moves between devices by JAX's collectives and lax.ppermute only.
A program may use at most 192 MiB of HBM per device.

```python
import math
import jax
import jax.numpy as jnp
from jax import lax

B = 2048
TILE = 128
TILES = 16
STEPS = 4


def symmetric_part(noise):
    return (noise + jnp.swapaxes(noise, -1, -2)) * 0.7071067811865476


def draw_inv_local(key, part):
    key = jax.random.fold_in(key, 11)
    first_key, second_key = jax.random.split(key)
    noise = jax.random.normal(first_key, (STEPS, B, B), jnp.float32)
    levels_diag = jnp.exp(jax.random.uniform(second_key, (STEPS, B), jnp.float32, math.log(0.2), math.log(0.8)))
    return symmetric_part(noise) * (0.15 * B ** (-0.5)) + levels_diag[..., None] * jnp.eye(B, dtype=jnp.float32)


def draw_coupling(key, part):
    key = jax.random.fold_in(key, 23)
    noise = jax.random.normal(key, (STEPS, B, B), jnp.float32)
    return noise * (0.9 * B ** (-0.5))


def draw_tail_block(key, part):
    key = jax.random.fold_in(key, 37)
    first_key, second_key = jax.random.split(key)
    noise = jax.random.normal(first_key, (B, B), jnp.float32)
    levels_diag = jnp.exp(jax.random.uniform(second_key, (B,), jnp.float32, math.log(1.0), math.log(3.0)))
    return symmetric_part(noise) * (0.3 * B ** (-0.5)) + levels_diag[:, None] * jnp.eye(B, dtype=jnp.float32)


def with_ends(array, stream_key, low, largest):
    longest = array.shape.index(max(array.shape))
    spots = []
    for shift in (0, 1):
        where = [jax.random.randint(jax.random.fold_in(stream_key, axis), (), 0, length) for axis, length in enumerate(array.shape)]
        where[longest] = (where[longest] + shift) % array.shape[longest]
        spots.append(tuple(where))
    return array.at[spots[0]].set(low).at[spots[1]].set(largest)


def setup_inputs(seed: int = 0) -> dict:
    arg_keys = jax.random.split(jax.random.key(seed), 5)
    return {
        "inv_local": draw_inv_local(jax.random.fold_in(arg_keys[4], 71), 0),
        "coupling": draw_coupling(jax.random.fold_in(arg_keys[4], 71), 0),
        "tail_block": draw_tail_block(jax.random.fold_in(arg_keys[4], 71), 0),
        "adjacency": with_ends((jax.random.randint(arg_keys[3], (TILES, TILES), 0, 2) < 1).astype(jnp.int32), jax.random.fold_in(arg_keys[3], 1), 0, 1),
    }


def expand_tiles(adjacency):
    count = adjacency.shape[0]
    joined = jnp.maximum(adjacency, jnp.eye(count, dtype=jnp.int32))
    return jnp.repeat(jnp.repeat(joined, TILE, axis=0), TILE, axis=1).astype(jnp.float32)


def reference(inv_local, coupling, tail_block, adjacency):
    tile_mask = expand_tiles(adjacency)
    highest = lax.Precision.HIGHEST

    def sweep_step(later, blocks):
        local_block, coupling_block = blocks
        cross = jnp.dot(later, coupling_block, precision=highest)
        current = local_block + jnp.dot(coupling_block.T, cross, precision=highest)
        return current, (current * tile_mask, -cross * tile_mask)

    _, (sel_diag, sel_off) = lax.scan(sweep_step, tail_block, (inv_local, coupling), reverse=True)
    return sel_diag, sel_off
```

```python
import functools

import jax
import jax.numpy as jnp
import numpy as np
from jax import lax
from jax.experimental import pallas as pl
from jax.experimental.pallas import tpu as pltpu
from jax.sharding import Mesh, PartitionSpec as P

TILE = 128
AXES = ("xh", "co", "z", "y", "xl")
SIZES = (2, 2, 4, 4, 2)


def route(place):
    pairs = []
    for i in range(int(np.prod(SIZES))):
        xh, co, z, y, xl = (int(v) for v in np.unravel_index(i, SIZES))
        at = place(x=2 * xh + xl, y=y, z=z, co=co, t=2 * xh + co, xl=xl)
        to = (at["x"] // 2, at["co"], at["z"], at["y"], at["x"] % 2)
        pairs.append((i, int(np.ravel_multi_index(to, SIZES))))
    assert len({b for _, b in pairs}) == len(pairs)
    return pairs


def send(x, place):
    return lax.ppermute(x, AXES, route(place))


def shifted(axis, by):
    def place(**at):
        return {**at, axis: (at[axis] + by) % 4}

    return place


def to_other_core(**at):
    return {**at, "co": 1 - at["co"]}


def panel_route(by):
    def place(x, y, z, co, t, xl):
        j = (t - y - by) % 4
        return dict(x=j, y=y, z=z, co=xl) if t % 2 else dict(x=y, y=j, z=z, co=xl)

    return place


def lower_route(by):
    def place(x, y, z, co, t, xl):
        v = (t - by) % 4
        return dict(x=y, y=z, z=v, co=xl) if t % 2 else dict(x=z, y=y, z=v, co=xl)

    return place


def tail_route(x, y, z, co, t, xl):
    return dict(x=y, y=t, z=z, co=xl)


def diag_out_route(by):
    def place(x, y, z, co, t, xl):
        step = (x + y + by) % 4
        q = y if step % 2 else x
        return dict(x=2 * (step // 2) + co, co=step % 2, z=z, y=q)

    return place


def off_out_route(by):
    def place(x, y, z, co, t, xl):
        step = (x + y + by) % 4
        b = y if step % 2 else x
        return dict(x=2 * (step // 2) + co, co=step % 2, z=b, y=z)

    return place


def gathered(x, axis):
    return [x] + [send(x, shifted(axis, -r)) for r in (1, 2, 3)]


def scattered(parts, axis):
    total = parts[0]
    for r in (1, 2, 3):
        total = total + send(parts[r], shifted(axis, r))
    return total


def split(x):
    hi = x.astype(jnp.bfloat16)
    lo = (x - hi.astype(jnp.float32)).astype(jnp.bfloat16)
    return hi, lo


def dot_cols(a, b):
    dims = (((0,), (0,)), ((), ()))
    mm = functools.partial(
        lax.dot_general, dimension_numbers=dims, preferred_element_type=jnp.float32
    )
    a_hi, a_lo = split(a)
    b_hi, b_lo = split(b)
    return mm(a_hi, b_hi) + (mm(a_hi, b_lo) + mm(a_lo, b_hi))


def first_kernel(at, t_own, t_sib, a_own, a_sib, o0, o1, o2, o3, y):
    p = at[0]
    y[...] = dot_cols(t_own[...], a_own[...]) + dot_cols(t_sib[...], a_sib[...])
    for r, o in enumerate((o0, o1, o2, o3)):
        rows = pl.multiple_of(lax.rem(p + r, 4) * 128, 128)
        o[...] = y[pl.ds(rows, 128), :]


def cross_kernel(at, x_own, x_sib, a_own, a_sib, o0, o1, o2, o3, a, y):
    p, c, q = at[0], at[1], at[2]
    for r in range(4):
        src = pl.multiple_of(lax.rem(q + r, 4) * 64, 64)
        for ref, half in ((a_own, c), (a_sib, 1 - c)):
            rows = pl.multiple_of(128 * r + 64 * half, 64)
            a[pl.ds(rows, 64), :] = ref[pl.ds(src, 64), :]
    for ref, half in ((x_own, c), (x_sib, 1 - c)):
        rows = pl.multiple_of(256 * half, 256)
        y[pl.ds(rows, 256), :] = dot_cols(ref[...], a[...])
    for r, o in enumerate((o0, o1, o2, o3)):
        rows = pl.multiple_of(lax.rem(p + r, 4) * 128, 128)
        o[...] = y[pl.ds(rows, 128), :]


def close_kernel(at, y0, y1, y2, y3, b_own, b_sib, o0, o1, o2, o3, b, y, x):
    p, c, q = at[0], at[1], at[2]
    for r, piece in enumerate((y0, y1, y2, y3)):
        y[pl.ds(128 * r, 128), :] = piece[...]
        src = pl.multiple_of(lax.rem(p + r, 4) * 64, 64)
        for ref, half in ((b_own, c), (b_sib, 1 - c)):
            rows = pl.multiple_of(128 * r + 64 * half, 64)
            b[pl.ds(rows, 64), :] = ref[pl.ds(src, 64), :]
    x[...] = dot_cols(b[...], y[...])
    for r, o in enumerate((o0, o1, o2, o3)):
        rows = pl.multiple_of(lax.rem(q + r, 4) * 128, 128)
        o[...] = x[pl.ds(rows, 128), :]


def call(kernel, at, args, scratch):
    vmem = pl.BlockSpec(memory_space=pltpu.VMEM)
    return pl.pallas_call(
        kernel,
        out_shape=[jax.ShapeDtypeStruct((128, 256), jnp.float32)] * 4,
        in_specs=[pl.BlockSpec(memory_space=pltpu.SMEM)] + [vmem] * len(args),
        out_specs=[vmem] * 4,
        scratch_shapes=[pltpu.VMEM(s, jnp.float32) for s in scratch],
        compiler_params=pltpu.CompilerParams(vmem_limit_bytes=24 * 1024 * 1024),
        cost_estimate=pl.CostEstimate(
            flops=6 * 512 * 512 * 256, bytes_accessed=2 << 20, transcendentals=0
        ),
    )(at, *args)


def on_device(inv_local, coupling, tail_block, adjacency):
    xh, co, z, y, xl = (lax.axis_index(a) for a in AXES)
    x = 2 * xh + xl
    t_own = 2 * xh + co
    local, factor, tail = inv_local[0], coupling[0], tail_block
    spot = {"x": x, "y": y, "z": z}

    def block(a, j):
        return lax.dynamic_slice(a, (0, 512 * j), (64, 512))

    def half(a, h):
        return jnp.where(h == 0, a[..., :256], a[..., 256:])

    def pick(stack, i):
        return lax.dynamic_index_in_dim(stack, i, 0, keepdims=False)

    tail_piece = send(block(tail, t_own), tail_route)
    upper = jnp.stack([send(block(factor, (t_own - y - r) % 4), panel_route(r)) for r in range(4)])
    lower = jnp.stack([send(block(factor, (t_own - r) % 4), lower_route(r)) for r in range(4)])
    locals_ = jnp.stack([send(block(local, (t_own - y - r) % 4), panel_route(r)) for r in range(4)])

    swapped = send(half(locals_, 1 - co), to_other_core)
    kept = half(locals_, co)
    low = jnp.where(co == 0, kept, swapped)
    high = jnp.where(co == 0, swapped, kept)
    local_pieces = jnp.concatenate([low, high], axis=1)

    def ring(steps, axis, source, where):
        mine = jnp.stack([pick(source, where(t)) for t in steps])
        pieces = gathered(mine, axis)
        return jnp.stack(pieces, axis=1)

    def canonical(rel, axis):
        q = spot[axis]
        order = [(i - q) % 4 for i in range(4)]
        return jnp.stack([pick(rel, o) for o in order])

    at_upper = lambda t: (t - x - y) % 4
    at_lower = lambda t: (t - z) % 4
    x3 = ring([3], "y", upper, at_upper)
    y3 = ring([3], "x", lower, at_lower)
    on_x = ring([2, 0], "x", upper, at_upper), ring([1], "x", lower, at_lower)
    on_y = ring([1], "y", upper, at_upper), ring([2, 0], "y", lower, at_lower)
    uppers = {3: (x3[0], "y"), 2: (on_x[0][0], "x"), 1: (on_y[0][0], "y"), 0: (on_x[0][1], "x")}
    lowers = {3: (y3[0], "x"), 2: (on_y[1][0], "y"), 1: (on_x[1][0], "x"), 0: (on_y[1][1], "y")}

    crosses, blocks = {}, {}
    current = None
    for t in (3, 2, 1, 0):
        first, second = ("y", "x") if t % 2 else ("x", "y")
        rel, axis = uppers[t]
        whole = canonical(rel, axis).reshape(256, 512)
        a_own = half(whole, co)
        a_sib = send(half(whole, 1 - co), to_other_core)
        rel, axis = lowers[t]
        b_own = canonical(rel, axis).reshape(256, 512)
        b_sib = send(b_own, to_other_core)
        at = jnp.stack([z, co, spot[second]]).astype(jnp.int32)
        if t == 3:
            pieces = jnp.stack(gathered(tail_piece, "x"))
            x_own = canonical(pieces, "x").reshape(256, 512)
            x_sib = send(x_own, to_other_core)
            parts = call(first_kernel, at, [x_own, x_sib, a_own, a_sib], [(512, 256)])
        else:
            x_own = jnp.concatenate(gathered(current, second))
            x_sib = send(x_own, to_other_core)
            parts = call(
                cross_kernel, at, [x_own, x_sib, a_own, a_sib], [(512, 256), (512, 256)]
            )
        cross = scattered(parts, "z")
        crosses[t] = cross
        at = jnp.stack([z, co, spot[first]]).astype(jnp.int32)
        parts = call(
            close_kernel,
            at,
            gathered(cross, "z") + [b_own, b_sib],
            [(512, 512), (512, 256), (512, 256)],
        )
        current = scattered(parts, first) + pick(local_pieces, (t - x - y) % 4)
        blocks[t] = current

    def panels(by_step):
        both = jnp.stack([by_step[t] for t in range(4)])
        top, bottom = both[:, :64], both[:, 64:]
        kept = jnp.where(co == 0, top, bottom)
        got = send(jnp.where(co == 0, bottom, top), to_other_core)
        left = jnp.where(co == 0, kept, got)
        right = jnp.where(co == 0, got, kept)
        return jnp.concatenate([left, right], axis=2)

    def placed(by_step, out_route, row):
        stack = panels(by_step)
        got = jnp.stack([send(pick(stack, (x + y + r) % 4), out_route(r)) for r in range(4)])
        return jnp.concatenate([pick(got, (t_own - row - j) % 4) for j in range(4)], axis=1)

    count = adjacency.shape[0]
    joined = jnp.maximum(adjacency, jnp.eye(count, dtype=jnp.int32)).astype(jnp.float32)
    tile_row = (z * 8 + y * 2 + xl) * 64 // TILE
    mask = jnp.repeat(pick(joined, tile_row), TILE)[None, :]
    sel_off = -placed(crosses, off_out_route, z) * mask
    sel_diag = placed(blocks, diag_out_route, y) * mask
    return sel_diag[None], sel_off[None]


def solution(mesh):
    fine = Mesh(mesh.devices.reshape(SIZES), AXES)
    rows = P(("xh", "co"), ("z", "y", "xl"), None)
    return jax.shard_map(
        on_device,
        mesh=fine,
        in_specs=(rows, rows, P(("z", "y", "xl"), None), P()),
        out_specs=(rows, rows),
        check_vma=False,
    )
```

```python
import functools

import jax
import jax.numpy as jnp
import numpy as np
from jax import lax
from jax.experimental import pallas as pl
from jax.experimental.pallas import tpu as pltpu
from jax.sharding import Mesh, PartitionSpec as P

TILE = 128
AXES = ("xh", "co", "z", "y", "xl")
SIZES = (2, 2, 4, 4, 2)
X, Y, Z, C, XL, ZH, LANE = range(7)


def route(place, only=None):
    pairs = []
    for i in range(int(np.prod(SIZES))):
        xh, co, z, y, xl = (int(v) for v in np.unravel_index(i, SIZES))
        at = dict(x=2 * xh + xl, y=y, z=z, co=co)
        if only is not None and not only(**at):
            continue
        at = place(**at)
        to = (at["x"] // 2, at["co"], at["z"], at["y"], at["x"] % 2)
        pairs.append((i, int(np.ravel_multi_index(to, SIZES))))
    assert len({b for _, b in pairs}) == len(pairs)
    return pairs


def send(x, place, only=None):
    return lax.ppermute(x, AXES, route(place, only))


def shifted(axis, by):
    def place(**at):
        return {**at, axis: (at[axis] + by) % 4}

    return place


def to_other_core(**at):
    return {**at, "co": 1 - at["co"]}


def deal(by):
    def place(**at):
        axis = "z" if at["co"] else "y"
        return {**at, axis: (at[axis] + by) % 4}

    return place


def x_pair(**at):
    return {**at, "x": at["x"] ^ 1}


def gathered(x, axis):
    return [x] + [send(x, shifted(axis, -r)) for r in (1, 2, 3)]


def scattered(parts, axis):
    total = parts[0]
    for r in (1, 2, 3):
        total = total + send(parts[r], shifted(axis, r))
    return total


def split(x):
    hi = x.astype(jnp.bfloat16)
    lo = (x - hi.astype(jnp.float32)).astype(jnp.bfloat16)
    return hi, lo


def dot_cols(a, b):
    dims = (((0,), (0,)), ((), ()))
    mm = functools.partial(
        lax.dot_general, dimension_numbers=dims, preferred_element_type=jnp.float32
    )
    a_hi, a_lo = split(a)
    b_hi, b_lo = split(b)
    return mm(a_hi, b_hi) + (mm(a_hi, b_lo) + mm(a_lo, b_hi))


def dot_rows(a, b_hi, b_lo):
    a_hi, a_lo = split(a)
    mm = functools.partial(jnp.dot, preferred_element_type=jnp.float32)
    return mm(a_hi, b_hi) + (mm(a_hi, b_lo) + mm(a_lo, b_hi))


def put_parts(value, turn_by, outs):
    for r, o in enumerate(outs):
        rows = pl.multiple_of(lax.rem(turn_by + r, 4) * 128, 128)
        o[...] = value[pl.ds(rows, 128), :]


def cross_of(at, x_own, x_sib, a, y, outs):
    p, c = at[Z], at[C]
    for ref, half in ((x_own, c), (x_sib, 1 - c)):
        rows = pl.multiple_of(256 * half, 256)
        y[pl.ds(rows, 256), :] = dot_cols(ref[...], a[...])
    put_parts(y, p, outs)


def cross_tail_kernel(at, t_own, t_one, t_two, a0, a1, a2, a3, o0, o1, o2, o3, a, y):
    c, q, even = at[C], at[Y], at[XL]
    for r, piece in enumerate((a0, a1, a2, a3)):
        rows = pl.multiple_of(lax.rem(q + r, 4) * 128, 128)
        a[pl.ds(rows, 128), :] = piece[...]
    a_hi, a_lo = split(a[...])

    def put(rows_of, count, first, half):
        part = dot_rows(rows_of[...].reshape(count * 64, 512), a_hi, a_lo)
        for i in range(count):
            rows = pl.multiple_of(128 * (first + i) + 64 * half, 64)
            y[pl.ds(rows, 64), :] = part[64 * i : 64 * i + 64]

    put(t_own, 4, 0, even)
    put(t_one, 2, 2 * c, 1 - even)
    put(t_two, 2, 2 * (1 - c), 1 - even)
    put_parts(y, at[Z], (o0, o1, o2, o3))


def cross_even_kernel(which, at, x_own, x_sib, a_all, o0, o1, o2, o3, a, y):
    q, c = at[Y], at[C]
    for r in range(4):
        a[pl.ds(128 * r, 128), :] = a_all[2 * lax.rem(q + r, 4) + c, which]
    cross_of(at, x_own, x_sib, a, y, (o0, o1, o2, o3))


def cross_odd_kernel(at, x_own, x_sib, a_all, o0, o1, o2, o3, a, y):
    q, c = at[X], at[C]
    for r in range(4):
        for h in range(2):
            a[pl.ds(128 * r, 128), pl.ds(128 * h, 128)] = a_all[2 * lax.rem(q + r, 4) + c, h]
    cross_of(at, x_own, x_sib, a, y, (o0, o1, o2, o3))


def close_odd_kernel(which, at, y0, y1, y2, y3, b_all, o0, o1, o2, o3, b, y, x):
    p, q = at[Z], at[Y]
    for r, piece in enumerate((y0, y1, y2, y3)):
        y[pl.ds(128 * r, 128), :] = piece[...]
        for h in range(2):
            b[pl.ds(128 * r, 128), pl.ds(256 * h, 256)] = b_all[2 * lax.rem(p + r, 4) + h, which]
    x[...] = dot_cols(b[...], y[...])
    put_parts(x, q, (o0, o1, o2, o3))


def close_even_kernel(skip, at, y0, y1, y2, y3, b_all, o0, o1, o2, o3, b, y, x):
    p, q, h = at[Z], at[X], at[ZH]
    for r, piece in enumerate((y0, y1, y2, y3)):
        y[pl.ds(128 * r, 128), :] = piece[...]
        for j in range(4):
            block = b_all[2 * j + h, skip + lax.rem(p + r, 4)]
            b[pl.ds(128 * r, 128), pl.ds(128 * j, 128)] = block
    x[...] = dot_cols(b[...], y[...])
    put_parts(x, q, (o0, o1, o2, o3))


def deal_kernel(at, factor, local, tail, *outs):
    for r, out in enumerate(outs):
        for k in range(4):
            v = lax.rem(at[LANE] + r, 4)
            col = jnp.where(at[C] == 0, 512 * k + 128 * v, 512 * v + 128 * k)
            cols = pl.ds(pl.multiple_of(col, 128), 128)
            out[0, :, pl.ds(128 * k, 128)] = factor[:, cols]
            out[1, :, pl.ds(128 * k, 128)] = jnp.where(at[C] == 0, local[:, cols], tail[:, cols])


def pair_kernel(at, d0, d1, d2, d3, factor, local, keep, give):
    low, high = pl.ds(0, 256), pl.ds(256, 256)

    @pl.when(at[C] == 0)
    def _():
        for r, d in enumerate((d0, d1, d2, d3)):
            s = lax.rem(at[LANE] + 4 - r, 4)
            for k in range(2):
                keep[s, k] = d[k, :, low]
                give[s, k] = d[k, :, high]
        for s in range(4):
            for k in range(2, 5):
                give[s, k] = jnp.zeros((64, 256), jnp.float32)
                keep[s, k] = jnp.zeros((64, 256), jnp.float32)

    @pl.when(at[C] == 1)
    def _():
        for r, d in enumerate((d0, d1, d2, d3)):
            s = lax.rem(at[LANE] + 4 - r, 4)
            keep[s, 1] = d[0, :, high]
            give[s, 1] = d[0, :, low]
            for h, cols in enumerate((low, high)):
                keep[s, 3 + h] = d[1, :, cols]
                give[s, 3 + h] = d[1, :, cols]
        for s in range(4):
            for k, ref in ((0, factor), (2, local)):
                for i in range(2):
                    here = pl.ds(128 * i, 128)
                    give[s, k, :, here] = ref[:, pl.ds(512 * i + 128 * s, 128)]
                    keep[s, k, :, here] = ref[:, pl.ds(512 * (i + 2) + 128 * s, 128)]


def row_kernel(at, keep, got, a0, a1, a2, a3, b0, b1, b2, b3, t_all, t_half):
    def fill(odd, even):
        for r, (a, b) in enumerate(((a0, b0), (a1, b1), (a2, b2), (a3, b3))):
            s = lax.rem(at[X] + r, 4)
            a[0], a[1] = odd[s, 0], odd[s, 1]
            b[0], b[1], b[2] = odd[s, 2], even[s, 0], even[s, 1]
        for s in range(4):
            for h in range(2):
                t_all[s, :, pl.ds(256 * h, 256)] = odd[s, 3 + h]
        for i in range(2):
            for h in range(2):
                t_half[i, :, pl.ds(256 * h, 256)] = odd[2 * at[C] + i, 3 + h]

    @pl.when(at[C] == 0)
    def _():
        fill(got, keep)

    @pl.when(at[C] == 1)
    def _():
        fill(keep, got)


def from_x(at, r):
    s = lax.rem(at[X] + 4 - r, 4)
    return s // 2, pl.ds(pl.multiple_of(64 * lax.rem(s, 2), 64), 64)


def base_kernel(at, a0, a1, a2, a3, upper_one, upper_three, lower):
    for r, a in enumerate((a0, a1, a2, a3)):
        step, rows = from_x(at, r)
        lower[step, rows, :] = a[1]

        @pl.when(step == 0)
        def _():
            upper_one[rows, :] = a[0]

        @pl.when(step == 1)
        def _():
            upper_three[rows, :] = a[0]


def rest_kernel(at, b0, b1, b2, b3, l0, l1, l2, l3, upper, same, other):
    for r, b in enumerate((b0, b1, b2, b3)):
        step, rows = from_x(at, r)
        upper[step, rows, :] = b[1]
        for n, (odd, even) in enumerate(((l1, l0), (l3, l2))):

            @pl.when(step == n)
            def _():
                odd[rows, :] = b[0]
                even[rows, :] = b[2]

        swap = lax.rem(at[Z], 2)
        here = pl.ds(pl.multiple_of(128 * swap, 128), 128)
        there = pl.ds(pl.multiple_of(128 * (1 - swap), 128), 128)
        same[step, rows, :] = b[1, :, here]
        other[step, rows, :] = b[1, :, there]


def column_kernel(at, e0, e1, e2, e3, upper, first, second):
    for h in range(2):
        first[h] = upper[:, pl.ds(128 * h, 128)]
    for r, e in enumerate((e0, e1, e2, e3)):
        s = lax.rem(at[Z] + 4 - r, 4)
        first[2 + s] = e[1]
        second[s] = e[0]


def leave_kernel(at, *refs):
    kept, outs = refs[:8], refs[8:]
    for r, out in enumerate(outs):
        for s in range(4):

            @pl.when(lax.rem(at[X] + r, 4) == s)
            def _():
                for n in range(2):
                    for k in range(2):
                        ref = kept[2 * (2 * (s // 2) + n) + k]
                        out[n, k] = ref[pl.ds(64 * (s % 2), 64), :]


def meet_kernel(at, a0, a1, a2, a3, keep, give):
    for r, a in enumerate((a0, a1, a2, a3)):
        s = lax.rem(at[X] + 4 - r, 4)
        keep[s] = a[at[C]]
        give[s] = a[1 - at[C]]


def turn_kernel(at, keep, got, *outs):
    mine = pl.ds(pl.multiple_of(256 * at[C], 256), 256)
    theirs = pl.ds(pl.multiple_of(256 * (1 - at[C]), 256), 256)
    for r, out in enumerate(outs):
        s = lax.rem(at[Y] + r, 4)
        for k in range(2):
            out[k, :, mine] = keep[s, k]
            out[k, :, theirs] = got[s, k]


def finish_kernel(at, mask, d0, d1, d2, d3, g1, g2, g3, diag, off):
    def fill(parts, sign):
        for r, part in enumerate(parts):
            s = lax.rem(at[Y] + 4 + sign * r, 4)
            for k in range(4):
                cols = pl.ds(pl.multiple_of(512 * k + 128 * s, 128), 128)
                kept = mask[4 * k + s]
                diag[:, cols] = part[0, :, pl.ds(128 * k, 128)] * kept
                off[:, cols] = -part[1, :, pl.ds(128 * k, 128)] * kept

    @pl.when(at[C] == 0)
    def _():
        fill((d0, g1, g2, g3), -1)

    @pl.when(at[C] == 1)
    def _():
        fill((d0, d1, d2, d3), 1)


def local(kernel, at, args, shapes, scratch=(), flops=0, scalars=()):
    vmem = pl.BlockSpec(memory_space=pltpu.VMEM)
    smem = pl.BlockSpec(memory_space=pltpu.SMEM)
    moved = sum(int(np.prod(a.shape)) for a in args) + sum(int(np.prod(s)) for s in shapes)
    return pl.pallas_call(
        kernel,
        out_shape=[jax.ShapeDtypeStruct(s, jnp.float32) for s in shapes],
        in_specs=[smem] * (1 + len(scalars)) + [vmem] * len(args),
        out_specs=[vmem] * len(shapes),
        scratch_shapes=[pltpu.VMEM(s, jnp.float32) for s in scratch],
        compiler_params=pltpu.CompilerParams(vmem_limit_bytes=32 * 1024 * 1024),
        cost_estimate=pl.CostEstimate(flops=flops, bytes_accessed=4 * moved, transcendentals=0),
    )(at, *scalars, *args)


def product(kernel, at, args, scratch):
    return local(kernel, at, args, [(128, 256)] * 4, scratch, flops=6 * 512 * 512 * 256)


def ring(pieces, place, only=None):
    return [pieces[0]] + [send(pieces[r], place(r), only) for r in (1, 2, 3)]


def after(values, done):
    return lax.optimization_barrier((tuple(values), done))[0]


def on_device(inv_local, coupling, tail_block, adjacency):
    xh, co, z, y, xl = (lax.axis_index(a) for a in AXES)
    x = 2 * xh + xl
    at = jnp.stack([x, y, z, co, xl, z // 2, jnp.where(co == 0, y, z)]).astype(jnp.int32)
    along = {axis: functools.partial(shifted, axis) for axis in "xyz"}

    factor, own, tail = coupling[0], inv_local[0], tail_block
    dealt = ring(local(deal_kernel, at, [factor, own, tail], [(2, 64, 512)] * 4), deal)
    keep, give = local(pair_kernel, at, dealt + [factor, own], [(4, 5, 64, 256)] * 2)
    got = send(give, to_other_core)
    *rows, t_all, t_half = local(
        row_kernel,
        at,
        [keep, got],
        [(2, 64, 256)] * 4 + [(3, 64, 256)] * 4 + [(4, 64, 512), (2, 64, 512)],
    )
    first = ring(rows[:4], along["x"])
    t_one = send(t_half, x_pair)
    t_two = send(t_one, to_other_core)
    upper_one, upper_three, lower_odd = local(
        base_kernel, at, first, [(128, 256), (128, 256), (2, 128, 256)]
    )
    on_x = lax.all_gather(lower_odd, ("xh", "xl", "co"))
    pieces = gathered(upper_three, "y")
    wide, square = (512, 256), (512, 512)
    parts = product(cross_tail_kernel, at, [t_all, t_one, t_two] + pieces, [wide, wide])

    rest = ring(after(rows[4:], parts[0]), along["x"])
    l0, l1, l2, l3, upper_even, same, other = local(
        rest_kernel, at, rest, [(128, 256)] * 4 + [(2, 128, 256)] + [(2, 128, 128)] * 2
    )
    locals_ = [l0, l1, l2, l3]
    cross = scattered(parts, "z")
    crosses, blocks = {3: cross}, {}

    on_x_even = lax.all_gather(upper_even, ("xh", "xl", "co"))
    same, other = after([same, other], cross)
    columns = [same]
    for r, block in ((1, other), (2, same), (3, other)):
        aimed = lambda z, co, **_: ((z + r) % 4) // 2 == co
        columns.append(send(block, along["z"](r), aimed))
    on_y, on_y_last = local(
        column_kernel, at, columns + [upper_one], [(6, 128, 128), (4, 128, 128)]
    )
    on_y = lax.all_gather(on_y, ("y", "co"))
    on_y_last = lax.all_gather(on_y_last, ("y", "co"))

    for t in (3, 2, 1, 0):
        first, second = ("y", "x") if t % 2 else ("x", "y")
        if t < 3:
            x_own = jnp.concatenate(gathered(blocks[t + 1], second))
            x_sib = send(x_own, to_other_core)
            if t % 2:
                kernel, a_all = cross_odd_kernel, on_y
            else:
                kernel, a_all = functools.partial(cross_even_kernel, t // 2), on_x_even
            cross = scattered(product(kernel, at, [x_own, x_sib, a_all], [wide, wide]), "z")
            crosses[t] = cross
        if t % 2:
            kernel, b_all = functools.partial(close_odd_kernel, t // 2), on_x
        else:
            kernel = functools.partial(close_even_kernel, 2 if t else 0)
            b_all = on_y if t else on_y_last
        parts = product(kernel, at, gathered(cross, "z") + [b_all], [square, wide, wide])
        blocks[t] = scattered(parts, first) + locals_[t]

    outs = [a[t] for t in range(4) for a in (blocks, crosses)]
    outs = ring(local(leave_kernel, at, outs, [(2, 2, 64, 256)] * 4), along["x"])
    keep, give = local(meet_kernel, at, outs, [(4, 2, 64, 256)] * 2)
    got = send(give, to_other_core)
    turned = local(turn_kernel, at, [keep, got], [(2, 64, 512)] * 4)
    back = ring(turned, along["y"], lambda co, **_: co == 0)

    count = adjacency.shape[0]
    joined = jnp.maximum(adjacency, jnp.eye(count, dtype=jnp.int32)).astype(jnp.float32)
    mask = lax.dynamic_index_in_dim(joined, (z * 8 + y * 2 + xl) * 64 // TILE, 0, keepdims=False)
    diag, off = local(
        finish_kernel, at, list(turned) + back[1:], [(64, 2048)] * 2, scalars=[mask]
    )
    return diag[None], off[None]


def solution(mesh):
    fine = Mesh(mesh.devices.reshape(SIZES), AXES)
    rows = P(("xh", "co"), ("z", "y", "xl"), None)
    return jax.shard_map(
        on_device,
        mesh=fine,
        in_specs=(rows, rows, P(("z", "y", "xl"), None), P()),
        out_specs=(rows, rows),
        check_vma=False,
    )
```

```python
import functools

import jax
import jax.numpy as jnp
import numpy as np
from jax import lax
from jax.experimental import pallas as pl
from jax.experimental.pallas import tpu as pltpu
from jax.sharding import Mesh, PartitionSpec as P

TILE = 128
AXES = ("xh", "co", "z", "y", "xl")
SIZES = (2, 2, 4, 4, 2)
X, Y, Z, C, XL, LANE = range(6)


def route(place, only=None):
    pairs = []
    for i in range(int(np.prod(SIZES))):
        xh, co, z, y, xl = (int(v) for v in np.unravel_index(i, SIZES))
        at = dict(x=2 * xh + xl, y=y, z=z, co=co)
        if only is not None and not only(**at):
            continue
        at = place(**at)
        to = (at["x"] // 2, at["co"], at["z"], at["y"], at["x"] % 2)
        pairs.append((i, int(np.ravel_multi_index(to, SIZES))))
    assert len({b for _, b in pairs}) == len(pairs)
    return pairs


def send(x, place, only=None):
    return lax.ppermute(x, AXES, route(place, only))


def partner(axis, r):
    def place(**at):
        return {**at, axis: at[axis] ^ r}

    return place


def deal(r):
    def place(**at):
        axis = "z" if at["co"] else "y"
        return {**at, axis: at[axis] ^ r}

    return place


def to_other_core(**at):
    return {**at, "co": 1 - at["co"]}


def exchanged(pieces, place, only=None):
    return [pieces[0]] + [send(pieces[r], place(r), only) for r in (1, 2, 3)]


def gathered(piece, axis):
    return exchanged([piece] * 4, functools.partial(partner, axis))


def scattered(parts, axis):
    got = exchanged(parts, functools.partial(partner, axis))
    return sum(a[:128] for a in got[1:]) + got[0][:128], got


def after(values, done):
    return lax.optimization_barrier((tuple(values), done))[0]


def split(x):
    hi = x.astype(jnp.bfloat16)
    lo = (x - hi.astype(jnp.float32)).astype(jnp.bfloat16)
    return hi, lo


def dot_cols(a, b):
    dims = (((0,), (0,)), ((), ()))
    mm = functools.partial(
        lax.dot_general, dimension_numbers=dims, preferred_element_type=jnp.float32
    )
    a_hi, a_lo = split(a)
    b_hi, b_lo = split(b)
    return mm(a_hi, b_hi) + (mm(a_hi, b_lo) + mm(a_lo, b_hi))


def dot_rows(a, b):
    mm = functools.partial(jnp.dot, preferred_element_type=jnp.float32)
    a_hi, a_lo = split(a)
    b_hi, b_lo = split(b)
    return mm(a_hi, b_hi) + (mm(a_hi, b_lo) + mm(a_lo, b_hi))


def rows_of(start, count):
    return pl.ds(pl.multiple_of(start, count), count)


def fetch(pairs, sems, first=0):
    copies = [
        pltpu.make_async_copy(a, b, sems.at[first + i]) for i, (a, b) in enumerate(pairs)
    ]
    for copy in copies:
        copy.start()
    return copies


def arrive(copies):
    for copy in copies:
        copy.wait()


def put_parts(value, place, outs):
    for r, o in enumerate(outs):
        o[pl.ds(0, 128), :] = value[rows_of(128 * (place ^ r), 128), :]


def put_pieces(pieces, place, ref):
    for r, piece in enumerate(pieces):
        ref[rows_of(128 * (place ^ r), 128), :] = piece[...]


def cross_tail_kernel(at, t_own, t_one, t_two, *rest):
    pieces, riders, outs, (a, y) = rest[:4], rest[4:8], rest[8:12], rest[12:]
    for o, rider in zip(outs, riders):
        o[pl.ds(128, 64), :] = rider[...]
    put_pieces(pieces, at[Y], a)

    def put(ref, count, first, half):
        part = dot_rows(ref[...].reshape(count * 64, 512), a[...])
        for i in range(count):
            y[rows_of(128 * (first + i) + 64 * half, 64), :] = part[64 * i : 64 * i + 64]

    put(t_own, 4, 0, at[XL])
    put(t_one, 2, 2 * at[C], 1 - at[XL])
    put(t_two, 2, 2 * (1 - at[C]), 1 - at[XL])
    put_parts(y, at[Z], outs)


def cross_kernel(odd, slot, at, a_all, *rest):
    halves, outs, (a, y, sems) = rest[:2], rest[2:6], rest[6:]
    c = at[C]
    place = at[X] if odd else at[Y]
    if odd:
        blocks = [
            (
                a_all.at[2 * (place ^ j) + c, 0, 2 * h + i],
                a.at[pl.ds(128 * j + 64 * i, 64), pl.ds(128 * h, 128)],
            )
            for j in range(4)
            for h in range(2)
            for i in range(2)
        ]
    else:
        blocks = [
            (
                a_all.at[2 * (place ^ j) + i, slot, rows_of(64 * c, 64), :],
                a.at[pl.ds(128 * j + 64 * i, 64), :],
            )
            for j in range(4)
            for i in range(2)
        ]
    copies = fetch(blocks, sems)
    arrive(copies)
    for ref, half in zip(halves, (c, 1 - c)):
        y[rows_of(256 * half, 256), :] = dot_cols(ref[...], a[...])
    put_parts(y, at[Z], outs)


def close_kernel(odd, slot, at, b_all, *rest):
    pieces, outs, (b, x, y, sems) = rest[:4], rest[4:8], rest[8:]
    if odd:
        blocks = [
            (
                b_all.at[2 * j + h, 1, pl.ds(64 * i, 64), :],
                b.at[2 * j + i, :, pl.ds(256 * h, 256)],
            )
            for j in range(4)
            for h in range(2)
            for i in range(2)
        ]
    else:
        blocks = [
            (b_all.at[2 * j + i, slot, k], b.at[2 * k + i, :, pl.ds(128 * j, 128)])
            for j in range(4)
            for i in range(2)
            for k in range(4)
        ]
    copies = fetch(blocks, sems)
    put_pieces(pieces, at[Z], y)
    arrive(copies)
    x[...] = dot_cols(b[...].reshape(512, 512), y[...])
    put_parts(x, at[Y] if odd else at[X], outs)


def close_ring_kernel(at, b_own, b_sib, y0, y1, y2, y3, *rest):
    outs, (b, x, y) = rest[:4], rest[4:]
    put_pieces((y0, y1, y2, y3), at[Z], y)
    for ref, half in ((b_own, at[C]), (b_sib, 1 - at[C])):
        for r in range(4):
            rows = rows_of(128 * (at[X] ^ r), 128)
            b[rows, rows_of(256 * half, 256)] = ref[pl.ds(128 * r, 128), :]
    x[...] = dot_cols(b[...], y[...])
    put_parts(x, at[Y], outs)


def deal_kernel(at, factor, local, tail, *rest):
    outs, sems = rest[:4], rest[4]

    def blocks(ref, n):
        pairs = []
        for r, out in enumerate(outs):
            for k in range(4):
                v = at[LANE] ^ r
                col = jnp.where(at[C] == 0, 512 * k + 128 * v, 512 * v + 128 * k)
                pairs.append((ref.at[:, rows_of(col, 128)], out.at[n, :, pl.ds(128 * k, 128)]))
        return pairs

    copies = fetch(blocks(factor, 0), sems)

    @pl.when(at[C] == 0)
    def _():
        arrive(fetch(blocks(local, 1), sems, 16))

    @pl.when(at[C] == 1)
    def _():
        arrive(fetch(blocks(tail, 1), sems, 16))

    arrive(copies)


def pair_kernel(at, d0, d1, d2, d3, factor, local, keep, give):
    low, high = pl.ds(0, 256), pl.ds(256, 256)
    dealt = (d0, d1, d2, d3)

    def factors(ref):
        for r, d in enumerate(dealt):
            ref[at[LANE] ^ r, 0] = d[0, :, low]
            ref[at[LANE] ^ r, 1] = d[0, :, high]

    def nothing(ref, slots):
        for s in range(4):
            for k in slots:
                ref[s, k] = jnp.zeros((64, 256), jnp.float32)

    @pl.when(at[C] == 0)
    def _():
        for r, d in enumerate(dealt):
            keep[at[LANE] ^ r, 2] = d[1, :, low]
            give[at[LANE] ^ r, 2] = d[1, :, high]
        for ref in (keep, give):
            nothing(ref, (3, 4))

        @pl.when(at[XL] == 0)
        def _():
            factors(keep)
            nothing(give, (0, 1))

        @pl.when(at[XL] == 1)
        def _():
            factors(give)
            nothing(keep, (0, 1))

    @pl.when(at[C] == 1)
    def _():
        for r, d in enumerate(dealt):
            s = at[LANE] ^ r
            keep[s, 1] = d[0, :, high]
            give[s, 1] = d[0, :, low]
            for h, cols in enumerate((low, high)):
                keep[s, 3 + h] = d[1, :, cols]
                give[s, 3 + h] = d[1, :, cols]
        for s in range(4):
            for k, ref in ((0, factor), (2, local)):
                for i in range(2):
                    here = pl.ds(128 * i, 128)
                    give[s, k, :, here] = ref[:, pl.ds(512 * i + 128 * s, 128)]
                    keep[s, k, :, here] = ref[:, pl.ds(512 * (i + 2) + 128 * s, 128)]


def row_kernel(at, keep, got, *outs):
    rows, locals_, t_all = outs[:4], outs[4:8], outs[8]

    def fill(odd, even):
        for r, (a, e) in enumerate(zip(rows, locals_)):
            s = at[X] ^ r
            for k in range(2):
                a[k] = odd[s, k]
                a[2 + k] = even[s, k]
            e[0] = odd[s, 2]
            e[1] = even[s, 2]
        for s in range(4):
            for h in range(2):
                t_all[s, :, pl.ds(256 * h, 256)] = odd[s, 3 + h]
        for i, a in enumerate((rows[1], rows[3])):
            for h in range(2):
                a[4 + h] = odd[2 * at[C] + i, 3 + h]

    @pl.when(at[C] == 0)
    def _():
        fill(got, keep)

    @pl.when(at[C] == 1)
    def _():
        fill(keep, got)


def base_kernel(at, a0, a1, a2, a3, *rest):
    uppers, lower, riders, t_one = rest[:2], rest[2], rest[3:7], rest[7]
    target, gathers, sems = rest[8:]
    for r, a in enumerate((a0, a1, a2, a3)):
        s = at[X] ^ r
        n = s // 2
        rows = rows_of(64 * lax.rem(s, 2), 64)

        @pl.when(n == 0)
        def _():
            uppers[0][rows, :] = a[0]
            gathers[1, rows, :] = a[1]

        @pl.when(n == 1)
        def _():
            uppers[1][rows, :] = a[0]
            lower[rows, :] = a[1]

        @pl.when(lax.rem(s, 2) == at[C])
        def _():
            for h in range(2):
                gathers[2 * (1 - n), pl.ds(64 * h, 64), :] = a[2 + h]
            for k, rider in enumerate(riders):
                v = at[Z] ^ k
                block = a[2 + v // 2, :, rows_of(128 * lax.rem(v, 2), 128)]
                rider[:, rows_of(128 * n, 128)] = block

    copies = fetch([(gathers, target)], sems)
    for i, a in enumerate((a1, a3)):
        for h in range(2):
            t_one[i, :, pl.ds(256 * h, 256)] = a[4 + h]
    arrive(copies)


def column_kernel(at, e0, e1, e2, e3, upper, target, out, sems):
    for h in range(2):
        for i in range(2):
            out[0, 2 * h + i] = upper[pl.ds(64 * i, 64), pl.ds(128 * h, 128)]
    for r, e in enumerate((e0, e1, e2, e3)):
        for n in range(2):
            out[1 + n, at[Z] ^ r] = e[pl.ds(128, 64), pl.ds(128 * n, 128)]
    arrive(fetch([(out, target)], sems))


def local_kernel(at, e0, e1, e2, e3, *outs):
    for r, e in enumerate((e0, e1, e2, e3)):
        s = at[X] ^ r
        for n in range(2):

            @pl.when(s // 2 == n)
            def _():
                rows = rows_of(64 * lax.rem(s, 2), 64)
                outs[2 * n][rows, :] = e[1]
                outs[2 * n + 1][rows, :] = e[0]


def leave_kernel(at, *refs):
    kept, outs = refs[:8], refs[8:]
    for r, out in enumerate(outs):
        for s in range(4):

            @pl.when((at[X] ^ r) == s)
            def _():
                for n in range(2):
                    for k in range(2):
                        ref = kept[2 * (2 * (s // 2) + n) + k]
                        out[n, k] = ref[pl.ds(64 * (s % 2), 64), :]


def meet_kernel(at, a0, a1, a2, a3, keep, give):
    for r, a in enumerate((a0, a1, a2, a3)):
        keep[at[X] ^ r] = a[at[C]]
        give[at[X] ^ r] = a[1 - at[C]]


def turn_kernel(at, keep, got, *outs):
    mine, theirs = rows_of(256 * at[C], 256), rows_of(256 * (1 - at[C]), 256)
    for r, out in enumerate(outs):
        for k in range(2):
            out[k, :, mine] = keep[at[Y] ^ r, k]
            out[k, :, theirs] = got[at[Y] ^ r, k]


def finish_kernel(at, mask, d0, d1, d2, d3, g1, g2, g3, diag, off):
    def fill(parts):
        for r, part in enumerate(parts):
            s = at[Y] ^ r
            for k in range(4):
                cols = rows_of(512 * k + 128 * s, 128)
                kept = mask[4 * k + s]
                diag[:, cols] = part[0, :, pl.ds(128 * k, 128)] * kept
                off[:, cols] = -part[1, :, pl.ds(128 * k, 128)] * kept

    @pl.when(at[C] == 0)
    def _():
        fill((d0, g1, g2, g3))

    @pl.when(at[C] == 1)
    def _():
        fill((d0, d1, d2, d3))


def local(kernel, at, args, shapes, scratch=(), copies=0, scalars=(), far=(), flops=0, out_far=0):
    vmem = pl.BlockSpec(memory_space=pltpu.VMEM)
    smem = pl.BlockSpec(memory_space=pltpu.SMEM)
    hbm = pl.BlockSpec(memory_space=pltpu.HBM)
    moved = sum(int(np.prod(a.shape)) for a in args) + sum(int(np.prod(s)) for s in shapes)
    scratch = [pltpu.VMEM(s, jnp.float32) for s in scratch]
    if copies:
        scratch.append(pltpu.SemaphoreType.DMA((copies,)))
    return pl.pallas_call(
        kernel,
        out_shape=[jax.ShapeDtypeStruct(s, jnp.float32) for s in shapes],
        in_specs=[smem] * (1 + len(scalars)) + [hbm] * len(far) + [vmem] * len(args),
        out_specs=[vmem] * (len(shapes) - out_far) + [hbm] * out_far,
        scratch_shapes=scratch,
        compiler_params=pltpu.CompilerParams(vmem_limit_bytes=16 * 1024 * 1024),
        cost_estimate=pl.CostEstimate(flops=flops, bytes_accessed=4 * moved, transcendentals=0),
    )(at, *scalars, *far, *args)


def product(kernel, at, args, scratch, rows=128, far=(), copies=0):
    work = 6 * 512 * 512 * 256
    return local(
        kernel, at, args, [(rows, 256)] * 4, scratch, copies=copies, far=far, flops=work
    )


def on_device(inv_local, coupling, tail_block, adjacency):
    xh, co, z, y, xl = (lax.axis_index(a) for a in AXES)
    x = 2 * xh + xl
    at = jnp.stack([x, y, z, co, xl, jnp.where(co == 0, y, z)]).astype(jnp.int32)
    along = {axis: functools.partial(partner, axis) for axis in "xyz"}
    piece, half_piece = (128, 256), (64, 256)
    wide, square = (512, 256), (512, 512)
    x8, y8 = ("xh", "xl", "co"), ("y", "co")

    factor, own, tail = coupling[0], inv_local[0], tail_block
    dealt = local(deal_kernel, at, [], [(2, 64, 512)] * 4, copies=32, far=[factor, own, tail])
    dealt = exchanged(dealt, deal)
    keep, give = local(pair_kernel, at, dealt + [factor, own], [(4, 5, 64, 256)] * 2)
    got = send(give, to_other_core)
    *rows, t_all = local(
        row_kernel,
        at,
        [keep, got],
        [(n, 64, 256) for n in (4, 6, 4, 6)] + [(2, 64, 256)] * 4 + [(4, 64, 512)],
    )
    rows, rows_local = rows[:4], rows[4:]
    (upper_one, upper_three, lower_three, *riders, t_one, on_x) = local(
        base_kernel,
        at,
        exchanged(rows, along["x"]),
        [piece] * 3 + [half_piece] * 4 + [(2, 64, 512)] + [(3, *piece)],
        [(3, *piece)],
        copies=1,
        out_far=1,
    )
    pieces = gathered(upper_three, "y")
    lowers = gathered(lower_three, "x")
    (t_aside,) = after([t_one], pieces[1])
    t_two = send(t_aside, to_other_core)
    pieces = list(after(pieces, tuple(lowers)))
    parts = product(
        cross_tail_kernel, at, [t_all, t_one, t_two] + pieces + riders, [wide, wide], 192
    )
    b_own = jnp.concatenate(lowers)
    b_sib = send(b_own, to_other_core)
    (on_x, *rows_local) = after([on_x] + rows_local, parts[0])
    on_x = lax.all_gather(on_x, x8)
    cross, columns = scattered(parts, "z")
    locals_ = local(local_kernel, at, exchanged(rows_local, along["x"]), [piece] * 4)
    crosses, blocks = {3: cross}, {}
    (on_y,) = local(
        column_kernel,
        at,
        columns + [upper_one],
        [(3, 4, 64, 128)],
        [(3, 4, 64, 128)],
        copies=1,
        out_far=1,
    )

    for t in (3, 2, 1, 0):
        odd = t % 2 == 1
        first, second = ("y", "x") if odd else ("x", "y")
        if t < 3:
            mine = gathered(blocks[t + 1], second)
            x_own = jnp.concatenate(mine)
            if t == 2:
                (on_y,) = after([on_y], (blocks[3], on_x))
                on_y = lax.all_gather(on_y, y8)
            args = [x_own, send(x_own, to_other_core)]
            kernel = functools.partial(cross_kernel, odd, 0 if t else 2)
            far, copies = (on_y, 16) if odd else (on_x, 8)
            parts = product(kernel, at, args, [wide, wide], 128, [far], copies)
            cross, _ = scattered(parts, "z")
            crosses[t] = cross
        args = gathered(cross, "z")
        if t == 3:
            args = [b_own, b_sib] + args
            parts = product(close_ring_kernel, at, args, [square, wide, wide])
        else:
            kernel = functools.partial(close_kernel, odd, 1 + t // 2)
            far, copies = (on_x, 16) if odd else (on_y, 32)
            parts = product(kernel, at, args, [(8, 64, 512), wide, wide], 128, [far], copies)
        blocks[t] = scattered(parts, first)[0] + locals_[t]

    outs = [a[t] for t in range(4) for a in (blocks, crosses)]
    outs = exchanged(local(leave_kernel, at, outs, [(2, 2, 64, 256)] * 4), along["x"])
    keep, give = local(meet_kernel, at, outs, [(4, 2, 64, 256)] * 2)
    got = send(give, to_other_core)
    turned = local(turn_kernel, at, [keep, got], [(2, 64, 512)] * 4)
    back = exchanged(turned, along["y"], lambda co, **_: co == 0)

    count = adjacency.shape[0]
    joined = jnp.maximum(adjacency, jnp.eye(count, dtype=jnp.int32)).astype(jnp.float32)
    mask = lax.dynamic_index_in_dim(joined, (z * 8 + y * 2 + xl) * 64 // TILE, 0, keepdims=False)
    diag, off = local(
        finish_kernel, at, list(turned) + back[1:], [(64, 2048)] * 2, scalars=[mask]
    )
    return diag[None], off[None]


def solution(mesh):
    fine = Mesh(mesh.devices.reshape(SIZES), AXES)
    rows = P(("xh", "co"), ("z", "y", "xl"), None)
    return jax.shard_map(
        on_device,
        mesh=fine,
        in_specs=(rows, rows, P(("z", "y", "xl"), None), P()),
        out_specs=(rows, rows),
        check_vma=False,
    )
```

```python
import functools

import jax
import jax.numpy as jnp
import numpy as np
from jax import lax
from jax.experimental import pallas as pl
from jax.experimental.pallas import tpu as pltpu
from jax.sharding import Mesh, PartitionSpec as P

TILE = 128
AXES = ("xh", "co", "z", "y", "xl")
SIZES = (2, 2, 4, 4, 2)
X, Y, Z, C, XL, LANE = range(6)


def route(place, only=None):
    pairs = []
    for i in range(int(np.prod(SIZES))):
        xh, co, z, y, xl = (int(v) for v in np.unravel_index(i, SIZES))
        at = dict(x=2 * xh + xl, y=y, z=z, co=co)
        if only is not None and not only(**at):
            continue
        at = place(**at)
        to = (at["x"] // 2, at["co"], at["z"], at["y"], at["x"] % 2)
        pairs.append((i, int(np.ravel_multi_index(to, SIZES))))
    assert len({b for _, b in pairs}) == len(pairs)
    return pairs


def send(x, place, only=None):
    return lax.ppermute(x, AXES, route(place, only))


def partner(axis, r):
    def place(**at):
        return {**at, axis: at[axis] ^ r}

    return place


def deal(r):
    def place(**at):
        axis = "z" if at["co"] else "y"
        return {**at, axis: at[axis] ^ r}

    return place


def to_other_core(**at):
    return {**at, "co": 1 - at["co"]}


def exchanged(pieces, place, only=None):
    return [pieces[0]] + [send(pieces[r], place(r), only) for r in (1, 2, 3)]


def gathered(piece, axis):
    return exchanged([piece] * 4, functools.partial(partner, axis))


def scattered(parts, axis):
    got = exchanged(parts, functools.partial(partner, axis))
    return sum(a[:128] for a in got[1:]) + got[0][:128], got


def after(values, done):
    return lax.optimization_barrier((tuple(values), done))[0]


def split(x):
    hi = x.astype(jnp.bfloat16)
    lo = (x - hi.astype(jnp.float32)).astype(jnp.bfloat16)
    return hi, lo


def dot_cols(a, b):
    dims = (((0,), (0,)), ((), ()))
    mm = functools.partial(
        lax.dot_general, dimension_numbers=dims, preferred_element_type=jnp.float32
    )
    a_hi, a_lo = split(a)
    b_hi, b_lo = split(b)
    return mm(a_hi, b_hi) + (mm(a_hi, b_lo) + mm(a_lo, b_hi))


def dot_rows(a, b):
    mm = functools.partial(jnp.dot, preferred_element_type=jnp.float32)
    a_hi, a_lo = split(a)
    b_hi, b_lo = split(b)
    return mm(a_hi, b_hi) + (mm(a_hi, b_lo) + mm(a_lo, b_hi))


def rows_of(start, count):
    return pl.ds(pl.multiple_of(start, count), count)


def fetch(pairs, sems, first=0):
    copies = [
        pltpu.make_async_copy(a, b, sems.at[first + i]) for i, (a, b) in enumerate(pairs)
    ]
    for copy in copies:
        copy.start()
    return copies


def arrive(copies):
    for copy in copies:
        copy.wait()


def put_parts(value, place, outs):
    for r, o in enumerate(outs):
        o[pl.ds(0, 128), :] = value[rows_of(128 * (place ^ r), 128), :]


def put_pieces(pieces, place, ref):
    for r, piece in enumerate(pieces):
        ref[rows_of(128 * (place ^ r), 128), :] = piece[pl.ds(0, 128), :]


def cross_tail_kernel(at, t_own, t_one, t_two, *rest):
    pieces, riders, outs, (a, y) = rest[:4], rest[4:8], rest[8:12], rest[12:]
    for o, rider in zip(outs, riders):
        o[pl.ds(128, 64), :] = rider[...]
    put_pieces(pieces, at[Y], a)

    def put(ref, count, first, half):
        part = dot_rows(ref[...].reshape(count * 64, 512), a[...])
        for i in range(count):
            y[rows_of(128 * (first + i) + 64 * half, 64), :] = part[64 * i : 64 * i + 64]

    put(t_own, 4, 0, at[XL])
    put(t_one, 2, 2 * at[C], 1 - at[XL])
    put(t_two, 2, 2 * (1 - at[C]), 1 - at[XL])
    put_parts(y, at[Z], outs)


def cross_even_kernel(at, x_own, x_sib, a_own, *rest):
    o0, o1, o2, o3, a, y = rest[-6:]
    for r in range(4):
        row = 128 * (at[X] ^ at[Y] ^ r)
        theirs = rest[0][r, pl.ds(128, 64), :] if len(rest) > 6 else x_sib[pl.ds(512 + 64 * r, 64), :]
        a[rows_of(row + 64 * at[C], 64), :] = a_own[r]
        a[rows_of(row + 64 * (1 - at[C]), 64), :] = theirs
    cross_of(at, x_own, x_sib, a, y, (o0, o1, o2, o3))


def cross_odd_kernel(at, x_own, x_sib, a0, a1, a2, a3, o0, o1, o2, o3, a, y):
    for r, piece in enumerate((a0, a1, a2, a3)):
        a[rows_of(128 * (at[X] ^ at[Y] ^ r), 128), :] = piece[pl.ds(128, 128), :]
    cross_of(at, x_own, x_sib, a, y, (o0, o1, o2, o3))


def cross_of(at, x_own, x_sib, a, y, outs):
    for ref, half in ((x_own, at[C]), (x_sib, 1 - at[C])):
        y[rows_of(256 * half, 256), :] = dot_cols(ref[pl.ds(0, 512), :], a[...])
    put_parts(y, at[Z], outs)


def close_odd_kernel(at, b0, b1, b2, b3, b_sib, y0, y1, y2, y3, *rest):
    outs, (b, x, y) = rest[:4], rest[4:]
    put_pieces((y0, y1, y2, y3), at[Z], y)
    for r, own in enumerate((b0, b1, b2, b3)):
        rows = rows_of(128 * (at[X] ^ r), 128)
        b[rows, rows_of(256 * at[C], 256)] = own[pl.ds(0, 128), :]
        b[rows, rows_of(256 * (1 - at[C]), 256)] = b_sib[r, pl.ds(0, 128), :]
    x[...] = dot_cols(b[...], y[...])
    put_parts(x, at[Y], outs)


def close_even_kernel(slot, at, b0, b1, b2, b3, b_sib, y0, y1, y2, y3, *rest):
    outs, (b, x, y) = rest[:4], rest[4:]
    put_pieces((y0, y1, y2, y3), at[Z], y)
    here = pl.ds(128 * slot, 128)
    for r, own in enumerate((b0, b1, b2, b3)):
        cols = rows_of(128 * (at[Y] ^ r), 128)
        for k in range(4):
            b[rows_of(128 * k + 64 * at[C], 64), cols] = own[pl.ds(64 * k, 64), here]
            b[rows_of(128 * k + 64 * (1 - at[C]), 64), cols] = b_sib[r, pl.ds(64 * k, 64), here]
    x[...] = dot_cols(b[...], y[...])
    put_parts(x, at[X], outs)


def pair_kernel(at, mask, d0, d1, d2, d3, factor, local, keep, give):
    low, high = pl.ds(0, 256), pl.ds(256, 256)
    dealt = (d0, d1, d2, d3)

    def factors(ref):
        for r, d in enumerate(dealt):
            ref[at[LANE] ^ r, 0] = d[0, :, low]
            ref[at[LANE] ^ r, 1] = d[0, :, high]

    def nothing(ref, slots):
        for s in range(4):
            for k in slots:
                ref[s, k] = jnp.zeros((64, 256), jnp.float32)

    @pl.when(at[C] == 0)
    def _():
        for r, d in enumerate(dealt):
            keep[at[LANE] ^ r, 2] = d[1, :, low]
            give[at[LANE] ^ r, 2] = d[1, :, high]
        for ref in (keep, give):
            nothing(ref, (3, 4))

        @pl.when(at[XL] == 0)
        def _():
            factors(keep)
            nothing(give, (0, 1))

        @pl.when(at[XL] == 1)
        def _():
            factors(give)
            nothing(keep, (0, 1))

    @pl.when(at[C] == 1)
    def _():
        for r, d in enumerate(dealt):
            s = at[LANE] ^ r
            keep[s, 1] = d[0, :, high]
            give[s, 1] = d[0, :, low]
            for h, cols in enumerate((low, high)):
                keep[s, 3 + h] = d[1, :, cols]
                give[s, 3 + h] = d[1, :, cols]
        for s in range(4):
            for k, ref in ((0, factor), (2, local)):
                for i in range(2):
                    here = pl.ds(128 * i, 128)
                    give[s, k, :, here] = ref[:, pl.ds(512 * i + 128 * s, 128)]
                    keep[s, k, :, here] = ref[:, pl.ds(512 * (i + 2) + 128 * s, 128)]


def row_kernel(at, keep, got, *outs):
    rows, locals_, t_all = outs[:4], outs[4:8], outs[8]

    def fill(odd, even):
        for r, (a, e) in enumerate(zip(rows, locals_)):
            s = at[X] ^ r
            for k in range(2):
                a[k] = odd[s, k]
                a[2 + k] = even[s, k]
            e[0] = odd[s, 2]
            e[1] = even[s, 2]
        for s in range(4):
            for h in range(2):
                t_all[s, :, pl.ds(256 * h, 256)] = odd[s, 3 + h]
        for i, a in enumerate((rows[1], rows[3])):
            for h in range(2):
                a[4 + h] = odd[2 * at[C] + i, 3 + h]

    @pl.when(at[C] == 0)
    def _():
        fill(got, keep)

    @pl.when(at[C] == 1)
    def _():
        fill(keep, got)


def base_kernel(at, a0, a1, a2, a3, l0, l1, l2, l3, *outs):
    uppers, mixed, lower, riders, messages, t_one = (*outs[:3], outs[3:7], outs[7:11], outs[11])
    for out, rows in zip(messages, (l0, l1, l2, l3)):
        out[0] = rows[0]
        out[1] = rows[1]
    for r, a in enumerate((a0, a1, a2, a3)):
        s = at[X] ^ r
        n = s // 2
        rows = rows_of(64 * lax.rem(s, 2), 64)
        for i in range(2):

            @pl.when(n == i)
            def _():
                uppers[rows_of(128 * (1 - i) + 64 * lax.rem(s, 2), 64), :] = a[0]
                (mixed, lower)[i][rows, :] = a[1]

        @pl.when((n == 0) & (lax.rem(s, 2) == at[C]))
        def _():
            for h in range(2):
                mixed[pl.ds(128 + 64 * h, 64), :] = a[2 + h]

        @pl.when((n == 1) & (lax.rem(s, 2) == at[C]))
        def _():
            for out in messages:
                for h in range(2):
                    out[2 + h] = a[2 + h]

        @pl.when(lax.rem(s, 2) == at[C])
        def _():
            for k, rider in enumerate(riders):
                v = at[Z] ^ k
                block = a[2 + v // 2, :, rows_of(128 * lax.rem(v, 2), 128)]
                rider[:, rows_of(128 * n, 128)] = block

    for i, a in enumerate((a1, a3)):
        for h in range(2):
            t_one[i, :, pl.ds(256 * h, 256)] = a[4 + h]


def share_kernel(at, a0, a1, a2, a3, give, a_own):
    for r, a in enumerate((a0, a1, a2, a3)):
        give[r, pl.ds(0, 128), :] = a[pl.ds(0, 128), :]
        give[r, pl.ds(128, 64), :] = a[rows_of(128 + 64 * (1 - at[C]), 64), :]
        a_own[r] = a[rows_of(128 + 64 * at[C], 64), :]


def column_kernel(at, e0, e1, e2, e3, out):
    for r, e in enumerate((e0, e1, e2, e3)):
        out[rows_of(64 * (at[Z] ^ r), 64), :] = e[pl.ds(128, 64), :]


def local_kernel(at, e0, e1, e2, e3, *outs):
    a_own, a_give = outs[4:]
    for r, e in enumerate((e0, e1, e2, e3)):
        s = at[X] ^ r
        a_own[r] = e[2 + at[C]]
        a_give[pl.ds(64 * r, 64), :] = e[3 - at[C]]
        for n in range(2):

            @pl.when(s // 2 == n)
            def _():
                rows = rows_of(64 * lax.rem(s, 2), 64)
                outs[2 * n][rows, :] = e[1]
                outs[2 * n + 1][rows, :] = e[0]


def leave_kernel(at, *refs):
    kept, outs = refs[:8], refs[8:]
    for r, out in enumerate(outs):
        for s in range(4):

            @pl.when((at[X] ^ r) == s)
            def _():
                for n in range(2):
                    for k in range(2):
                        ref = kept[2 * (2 * (s // 2) + n) + k]
                        out[n, k] = ref[pl.ds(64 * (s % 2), 64), :]


def meet_kernel(at, a0, a1, a2, a3, keep, give):
    for r, a in enumerate((a0, a1, a2, a3)):
        keep[at[X] ^ r] = a[at[C]]
        give[at[X] ^ r] = a[1 - at[C]]


def turn_kernel(at, keep, got, *outs):
    mine, theirs = rows_of(256 * at[C], 256), rows_of(256 * (1 - at[C]), 256)
    for r, out in enumerate(outs):
        for k in range(2):
            out[k, :, mine] = keep[at[Y] ^ r, k]
            out[k, :, theirs] = got[at[Y] ^ r, k]


def finish_kernel(at, mask, d0, d1, d2, d3, g1, g2, g3, diag, off):
    def fill(parts):
        for r, part in enumerate(parts):
            s = at[Y] ^ r
            for k in range(4):
                cols = rows_of(512 * k + 128 * s, 128)
                kept = mask[4 * k + s]
                diag[:, cols] = part[0, :, pl.ds(128 * k, 128)] * kept
                off[:, cols] = -part[1, :, pl.ds(128 * k, 128)] * kept

    @pl.when(at[C] == 0)
    def _():
        fill((d0, g1, g2, g3))

    @pl.when(at[C] == 1)
    def _():
        fill((d0, d1, d2, d3))


def local(kernel, at, args, shapes, scratch=(), copies=0, scalars=(), far=(), flops=0, out_far=0):
    vmem = pl.BlockSpec(memory_space=pltpu.VMEM)
    smem = pl.BlockSpec(memory_space=pltpu.SMEM)
    hbm = pl.BlockSpec(memory_space=pltpu.HBM)
    moved = sum(int(np.prod(a.shape)) for a in args) + sum(int(np.prod(s)) for s in shapes)
    scratch = [pltpu.VMEM(s, jnp.float32) for s in scratch]
    if copies:
        scratch.append(pltpu.SemaphoreType.DMA((copies,)))
    return pl.pallas_call(
        kernel,
        out_shape=[jax.ShapeDtypeStruct(s, jnp.float32) for s in shapes],
        in_specs=[smem] * (1 + len(scalars)) + [hbm] * len(far) + [vmem] * len(args),
        out_specs=[vmem] * (len(shapes) - out_far) + [hbm] * out_far,
        scratch_shapes=scratch,
        compiler_params=pltpu.CompilerParams(vmem_limit_bytes=16 * 1024 * 1024),
        cost_estimate=pl.CostEstimate(flops=0, bytes_accessed=1024, transcendentals=0),
    )(at, *scalars, *far, *args)


def product(kernel, at, args, scratch, rows=128, far=(), copies=0):
    work = 6 * 512 * 512 * 256
    return local(
        kernel, at, args, [(rows, 256)] * 4, scratch, copies=copies, far=far, flops=work
    )


def on_device(inv_local, coupling, tail_block, adjacency):
    xh, co, z, y, xl = (lax.axis_index(a) for a in AXES)
    x = 2 * xh + xl
    at = jnp.stack([x, y, z, co, xl, jnp.where(co == 0, y, z)]).astype(jnp.int32)
    along = {axis: functools.partial(partner, axis) for axis in "xyz"}
    piece, half_piece = (128, 256), (64, 256)
    wide, square = (512, 256), (512, 512)
    x8, y8 = ("xh", "xl", "co"), ("y", "co")

    factor, own, tail = coupling[0], inv_local[0], tail_block
    lane = jnp.where(co == 0, y, z)

    def dealt_for(r):
        def columns(a):
            v = lane ^ r
            starts = [jnp.where(co == 0, 512 * k + 128 * v, 512 * v + 128 * k) for k in range(4)]
            return jnp.concatenate([lax.dynamic_slice(a, (0, s), (64, 128)) for s in starts], axis=1)

        return jnp.stack([columns(factor), jnp.where(co == 0, columns(own), columns(tail))])

    count = adjacency.shape[0]
    joined = jnp.maximum(adjacency, jnp.eye(count, dtype=jnp.int32)).astype(jnp.float32)
    mask = lax.dynamic_index_in_dim(joined, (z * 8 + y * 2 + xl) * 64 // TILE, 0, keepdims=False)
    dealt = exchanged([dealt_for(r) for r in range(4)], deal)
    keep, give = local(
        pair_kernel, at, dealt + [factor, own], [(4, 5, 64, 256)] * 2, scalars=[mask]
    )
    got = send(give, to_other_core)
    *rows, t_all = local(
        row_kernel,
        at,
        [keep, got],
        [(n, 64, 256) for n in (4, 6, 4, 6)] + [(2, 64, 256)] * 4 + [(4, 64, 512)],
    )
    rows, rows_local = rows[:4], rows[4:]
    (uppers, mixed, lower_three, *riders) = local(
        base_kernel,
        at,
        exchanged(rows, along["x"]) + rows_local,
        [(256, 256), (256, 256), piece]
        + [half_piece] * 4
        + [(4, 64, 256)] * 4
        + [(2, 64, 512)],
    )
    riders, rows_local, t_one = riders[:4], riders[4:8], riders[8]
    pieces = gathered(uppers, "y")
    lowers = gathered(lower_three, "x")
    (t_aside,) = after([t_one], pieces[1])
    t_two = send(t_aside, to_other_core)
    pieces = list(after(pieces, tuple(lowers)))
    parts = product(
        cross_tail_kernel, at, [t_all, t_one, t_two] + pieces + riders, [wide, wide], 192
    )
    b_sib = send(jnp.stack(lowers), to_other_core)
    rows_local = after(rows_local, parts[0])
    cross, columns = scattered(parts, "z")
    rows_local = exchanged(rows_local, along["x"])
    crosses, blocks = {3: cross}, {}
    (on_y,) = local(column_kernel, at, columns, [(256, 256)])

    for t in (3, 2, 1, 0):
        odd = t % 2 == 1
        first, second = ("y", "x") if odd else ("x", "y")
        if t < 3:
            mine = gathered(blocks[t + 1], second)
            if t == 2:
                (mixed,) = after([mixed], blocks[3])
                mixed = gathered(mixed, "x")
                x_own = jnp.concatenate(after(mine + [a_give], tuple(mixed)))
                (on_y,) = after([on_y], x_own)
                on_y = gathered(on_y, "y")
            else:
                x_own = jnp.concatenate(mine)
            args = [x_own, send(x_own, to_other_core)]
            if odd:
                args += pieces
            else:
                args += [a_own] if t else [a_own, b_sib]
            kernel = cross_odd_kernel if odd else cross_even_kernel
            parts = product(kernel, at, args, [wide, wide])
            cross, _ = scattered(parts, "z")
            crosses[t] = cross
        whole = gathered(cross, "z")
        if t == 2:
            on_y = list(after(on_y, tuple(whole)))
            on_y_sib = send(jnp.stack(on_y), to_other_core)
        args = list(lowers) + [b_sib] if odd else on_y + [on_y_sib]
        kernel = close_odd_kernel if odd else functools.partial(close_even_kernel, t // 2)
        args += whole
        parts = product(kernel, at, args, [square, wide, wide])
        if t == 3:
            rows_local = after(rows_local, parts[0])
            *locals_, a_own, a_give = local(
                local_kernel, at, rows_local, [piece] * 4 + [(4, *half_piece), (256, 256)]
            )
        if t == 2:
            lowers = list(after(mixed, parts[0]))
            give, a_own = local(share_kernel, at, lowers, [(4, 192, 256), (4, *half_piece)])
            b_sib = send(give, to_other_core)
        blocks[t] = scattered(parts, first)[0] + locals_[t]

    outs = [a[t] for t in range(4) for a in (blocks, crosses)]
    outs = exchanged(local(leave_kernel, at, outs, [(2, 2, 64, 256)] * 4), along["x"])
    keep, give = local(meet_kernel, at, outs, [(4, 2, 64, 256)] * 2)
    got = send(give, to_other_core)
    turned = local(turn_kernel, at, [keep, got], [(2, 64, 512)] * 4)
    back = exchanged(turned, along["y"], lambda co, **_: co == 0)

    diag, off = local(
        finish_kernel, at, list(turned) + back[1:], [(64, 2048)] * 2, scalars=[mask]
    )
    return diag[None], off[None]


def solution(mesh):
    fine = Mesh(mesh.devices.reshape(SIZES), AXES)
    rows = P(("xh", "co"), ("z", "y", "xl"), None)
    return jax.shard_map(
        on_device,
        mesh=fine,
        in_specs=(rows, rows, P(("z", "y", "xl"), None), P()),
        out_specs=(rows, rows),
        check_vma=False,
    )
```

```python
import functools

import jax
import jax.numpy as jnp
import numpy as np
from jax import lax
from jax.experimental import pallas as pl
from jax.experimental.pallas import tpu as pltpu
from jax.sharding import Mesh, PartitionSpec as P

TILE = 128
AXES = ("xh", "co", "z", "y", "xl")
SIZES = (2, 2, 4, 4, 2)
X, Y, Z, C, XL, LANE = range(6)


def route(place, only=None):
    pairs = []
    for i in range(int(np.prod(SIZES))):
        xh, co, z, y, xl = (int(v) for v in np.unravel_index(i, SIZES))
        at = dict(x=2 * xh + xl, y=y, z=z, co=co)
        if only is not None and not only(**at):
            continue
        at = place(**at)
        to = (at["x"] // 2, at["co"], at["z"], at["y"], at["x"] % 2)
        pairs.append((i, int(np.ravel_multi_index(to, SIZES))))
    assert len({b for _, b in pairs}) == len(pairs)
    return pairs


def send(x, place, only=None):
    return lax.ppermute(x, AXES, route(place, only))


def partner(axis, r):
    def place(**at):
        return {**at, axis: at[axis] ^ r}

    return place


def deal(r):
    def place(**at):
        axis = "z" if at["co"] else "y"
        return {**at, axis: at[axis] ^ r}

    return place


def to_other_core(**at):
    return {**at, "co": 1 - at["co"]}


def exchanged(pieces, place, only=None):
    return [pieces[0]] + [send(pieces[r], place(r), only) for r in (1, 2, 3)]


def gathered(piece, axis):
    return exchanged([piece] * 4, functools.partial(partner, axis))


def scattered(parts, axis):
    got = exchanged(parts, functools.partial(partner, axis))
    return sum(a[:128] for a in got[1:]) + got[0][:128], got


def after(values, done):
    return lax.optimization_barrier((tuple(values), done))[0]


def split(x):
    hi = x.astype(jnp.bfloat16)
    lo = (x - hi.astype(jnp.float32)).astype(jnp.bfloat16)
    return hi, lo


def dot_cols(a, b):
    dims = (((0,), (0,)), ((), ()))
    mm = functools.partial(
        lax.dot_general, dimension_numbers=dims, preferred_element_type=jnp.float32
    )
    a_hi, a_lo = split(a)
    b_hi, b_lo = split(b)
    return mm(a_hi, b_hi) + (mm(a_hi, b_lo) + mm(a_lo, b_hi))


def dot_rows(a, b):
    mm = functools.partial(jnp.dot, preferred_element_type=jnp.float32)
    a_hi, a_lo = split(a)
    b_hi, b_lo = split(b)
    return mm(a_hi, b_hi) + (mm(a_hi, b_lo) + mm(a_lo, b_hi))


def rows_of(start, count):
    return pl.ds(pl.multiple_of(start, count), count)


def fetch(pairs, sems, first=0):
    copies = [
        pltpu.make_async_copy(a, b, sems.at[first + i]) for i, (a, b) in enumerate(pairs)
    ]
    for copy in copies:
        copy.start()
    return copies


def arrive(copies):
    for copy in copies:
        copy.wait()


def put_parts(value, place, outs):
    for r, o in enumerate(outs):
        o[pl.ds(0, 128), :] = value[rows_of(128 * (place ^ r), 128), :]


def put_pieces(pieces, place, ref):
    for r, piece in enumerate(pieces):
        ref[rows_of(128 * (place ^ r), 128), :] = piece[pl.ds(0, 128), :]


def cross_tail_kernel(at, t_own, t_one, t_two, *rest):
    pieces, riders, outs, (a, y) = rest[:4], rest[4:8], rest[8:12], rest[12:]
    for o, rider in zip(outs, riders):
        o[pl.ds(128, 64), :] = rider[...]
    put_pieces(pieces, at[Y], a)

    def put(ref, count, first, half):
        part = dot_rows(ref[...].reshape(count * 64, 512), a[...])
        for i in range(count):
            y[rows_of(128 * (first + i) + 64 * half, 64), :] = part[64 * i : 64 * i + 64]

    put(t_own, 4, 0, at[XL])
    put(t_one, 2, 2 * at[C], 1 - at[XL])
    put(t_two, 2, 2 * (1 - at[C]), 1 - at[XL])
    put_parts(y, at[Z], outs)


def cross_even_kernel(at, x_own, x_sib, a_own, *rest):
    o0, o1, o2, o3, a, y = rest[-6:]
    for r in range(4):
        row = 128 * (at[X] ^ at[Y] ^ r)
        theirs = rest[0][r, pl.ds(128, 64), :] if len(rest) > 6 else x_sib[pl.ds(512 + 64 * r, 64), :]
        a[rows_of(row + 64 * at[C], 64), :] = a_own[r]
        a[rows_of(row + 64 * (1 - at[C]), 64), :] = theirs
    cross_of(at, x_own, x_sib, a, y, (o0, o1, o2, o3))


def cross_odd_kernel(at, x_own, x_sib, a0, a1, a2, a3, o0, o1, o2, o3, a, y):
    for r, piece in enumerate((a0, a1, a2, a3)):
        a[rows_of(128 * (at[X] ^ at[Y] ^ r), 128), :] = piece[pl.ds(128, 128), :]
    cross_of(at, x_own, x_sib, a, y, (o0, o1, o2, o3))


def cross_of(at, x_own, x_sib, a, y, outs):
    for ref, half in ((x_own, at[C]), (x_sib, 1 - at[C])):
        y[rows_of(256 * half, 256), :] = dot_cols(ref[pl.ds(0, 512), :], a[...])
    put_parts(y, at[Z], outs)


def close_odd_kernel(at, b0, b1, b2, b3, b_sib, y0, y1, y2, y3, *rest):
    outs, (b, x, y) = rest[:4], rest[4:]
    put_pieces((y0, y1, y2, y3), at[Z], y)
    for r, own in enumerate((b0, b1, b2, b3)):
        rows = rows_of(128 * (at[X] ^ r), 128)
        b[rows, rows_of(256 * at[C], 256)] = own[pl.ds(0, 128), :]
        b[rows, rows_of(256 * (1 - at[C]), 256)] = b_sib[r, pl.ds(0, 128), :]
    x[...] = dot_cols(b[...], y[...])
    put_parts(x, at[Y], outs)


def close_even_kernel(slot, at, b0, b1, b2, b3, b_sib, y0, y1, y2, y3, *rest):
    outs, (b, x, y) = rest[:4], rest[4:]
    put_pieces((y0, y1, y2, y3), at[Z], y)
    here = pl.ds(128 * slot, 128)
    for r, own in enumerate((b0, b1, b2, b3)):
        cols = rows_of(128 * (at[Y] ^ r), 128)
        for k in range(4):
            b[rows_of(128 * k + 64 * at[C], 64), cols] = own[pl.ds(64 * k, 64), here]
            b[rows_of(128 * k + 64 * (1 - at[C]), 64), cols] = b_sib[r, pl.ds(64 * k, 64), here]
    x[...] = dot_cols(b[...], y[...])
    put_parts(x, at[X], outs)


def pair_kernel(at, mask, d0, d1, d2, d3, factor, local, keep, give):
    low, high = pl.ds(0, 256), pl.ds(256, 256)
    dealt = (d0, d1, d2, d3)

    def factors(ref):
        for r, d in enumerate(dealt):
            ref[at[LANE] ^ r, 0] = d[0, :, low]
            ref[at[LANE] ^ r, 1] = d[0, :, high]

    def nothing(ref, slots):
        for s in range(4):
            for k in slots:
                ref[s, k] = jnp.zeros((64, 256), jnp.float32)

    @pl.when(at[C] == 0)
    def _():
        for r, d in enumerate(dealt):
            keep[at[LANE] ^ r, 2] = d[1, :, low]
            give[at[LANE] ^ r, 2] = d[1, :, high]
        for ref in (keep, give):
            nothing(ref, (3, 4))

        @pl.when(at[XL] == 0)
        def _():
            factors(keep)
            nothing(give, (0, 1))

        @pl.when(at[XL] == 1)
        def _():
            factors(give)
            nothing(keep, (0, 1))

    @pl.when(at[C] == 1)
    def _():
        for r, d in enumerate(dealt):
            s = at[LANE] ^ r
            keep[s, 1] = d[0, :, high]
            give[s, 1] = d[0, :, low]
            for h, cols in enumerate((low, high)):
                keep[s, 3 + h] = d[1, :, cols]
                give[s, 3 + h] = d[1, :, cols]
        for s in range(4):
            for k, ref in ((0, factor), (2, local)):
                for i in range(2):
                    here = pl.ds(128 * i, 128)
                    give[s, k, :, here] = ref[:, pl.ds(512 * i + 128 * s, 128)]
                    keep[s, k, :, here] = ref[:, pl.ds(512 * (i + 2) + 128 * s, 128)]


def row_kernel(at, keep, got, *outs):
    rows, locals_, t_all = outs[:4], outs[4:8], outs[8]

    def fill(odd, even):
        for r, (a, e) in enumerate(zip(rows, locals_)):
            s = at[X] ^ r
            for k in range(2):
                a[k] = odd[s, k]
                a[2 + k] = even[s, k]
            e[0] = odd[s, 2]
            e[1] = even[s, 2]
        for s in range(4):
            for h in range(2):
                t_all[s, :, pl.ds(256 * h, 256)] = odd[s, 3 + h]
        for i, a in enumerate((rows[1], rows[3])):
            for h in range(2):
                a[4 + h] = odd[2 * at[C] + i, 3 + h]

    @pl.when(at[C] == 0)
    def _():
        fill(got, keep)

    @pl.when(at[C] == 1)
    def _():
        fill(keep, got)


def base_kernel(at, a0, a1, a2, a3, *outs):
    uppers, mixed, riders, t_one = outs[0], outs[1:3], outs[3:7], outs[7]
    for r, a in enumerate((a0, a1, a2, a3)):
        s = at[X] ^ r
        n = s // 2
        rows = rows_of(64 * lax.rem(s, 2), 64)
        for i in range(2):

            @pl.when(n == i)
            def _():
                uppers[rows_of(128 * (1 - i) + 64 * lax.rem(s, 2), 64), :] = a[0]
                mixed[i][rows, :] = a[1]

            @pl.when((n == i) & (lax.rem(s, 2) == at[C]))
            def _():
                for h in range(2):
                    mixed[i][pl.ds(128 + 64 * h, 64), :] = a[2 + h]

        @pl.when(lax.rem(s, 2) == at[C])
        def _():
            for k, rider in enumerate(riders):
                v = at[Z] ^ k
                block = a[2 + v // 2, :, rows_of(128 * lax.rem(v, 2), 128)]
                rider[:, rows_of(128 * n, 128)] = block

    for i, a in enumerate((a1, a3)):
        for h in range(2):
            t_one[i, :, pl.ds(256 * h, 256)] = a[4 + h]


def share_kernel(at, a0, a1, a2, a3, give, a_own):
    for r, a in enumerate((a0, a1, a2, a3)):
        give[r, pl.ds(0, 128), :] = a[pl.ds(0, 128), :]
        give[r, pl.ds(128, 64), :] = a[rows_of(128 + 64 * (1 - at[C]), 64), :]
        a_own[r] = a[rows_of(128 + 64 * at[C], 64), :]


def column_kernel(at, e0, e1, e2, e3, out):
    for r, e in enumerate((e0, e1, e2, e3)):
        out[rows_of(64 * (at[Z] ^ r), 64), :] = e[pl.ds(128, 64), :]


def local_kernel(at, e0, e1, e2, e3, m0, m1, m2, m3, *outs):
    a_own, a_give = outs[4:]
    for r, m in enumerate((m0, m1, m2, m3)):
        a_own[r] = m[rows_of(128 + 64 * at[C], 64), :]
        a_give[pl.ds(64 * r, 64), :] = m[rows_of(128 + 64 * (1 - at[C]), 64), :]
    for r, e in enumerate((e0, e1, e2, e3)):
        s = at[X] ^ r
        for n in range(2):

            @pl.when(s // 2 == n)
            def _():
                rows = rows_of(64 * lax.rem(s, 2), 64)
                outs[2 * n][rows, :] = e[1]
                outs[2 * n + 1][rows, :] = e[0]


def leave_kernel(at, *refs):
    kept, outs = refs[:8], refs[8:]
    for r, out in enumerate(outs):
        for s in range(4):

            @pl.when((at[X] ^ r) == s)
            def _():
                for n in range(2):
                    for k in range(2):
                        ref = kept[2 * (2 * (s // 2) + n) + k]
                        out[n, k] = ref[pl.ds(64 * (s % 2), 64), :]


def meet_kernel(at, a0, a1, a2, a3, keep, give):
    for r, a in enumerate((a0, a1, a2, a3)):
        keep[at[X] ^ r] = a[at[C]]
        give[at[X] ^ r] = a[1 - at[C]]


def turn_kernel(at, keep, got, *outs):
    mine, theirs = rows_of(256 * at[C], 256), rows_of(256 * (1 - at[C]), 256)
    for r, out in enumerate(outs):
        for k in range(2):
            out[k, :, mine] = keep[at[Y] ^ r, k]
            out[k, :, theirs] = got[at[Y] ^ r, k]


def finish_kernel(at, mask, d0, d1, d2, d3, g1, g2, g3, diag, off):
    def fill(parts):
        for r, part in enumerate(parts):
            s = at[Y] ^ r
            for k in range(4):
                cols = rows_of(512 * k + 128 * s, 128)
                kept = mask[4 * k + s]
                diag[:, cols] = part[0, :, pl.ds(128 * k, 128)] * kept
                off[:, cols] = -part[1, :, pl.ds(128 * k, 128)] * kept

    @pl.when(at[C] == 0)
    def _():
        fill((d0, g1, g2, g3))

    @pl.when(at[C] == 1)
    def _():
        fill((d0, d1, d2, d3))


def local(kernel, at, args, shapes, scratch=(), copies=0, scalars=(), far=(), flops=0, out_far=0):
    vmem = pl.BlockSpec(memory_space=pltpu.VMEM)
    smem = pl.BlockSpec(memory_space=pltpu.SMEM)
    hbm = pl.BlockSpec(memory_space=pltpu.HBM)
    moved = sum(int(np.prod(a.shape)) for a in args) + sum(int(np.prod(s)) for s in shapes)
    scratch = [pltpu.VMEM(s, jnp.float32) for s in scratch]
    if copies:
        scratch.append(pltpu.SemaphoreType.DMA((copies,)))
    return pl.pallas_call(
        kernel,
        out_shape=[jax.ShapeDtypeStruct(s, jnp.float32) for s in shapes],
        in_specs=[smem] * (1 + len(scalars)) + [hbm] * len(far) + [vmem] * len(args),
        out_specs=[vmem] * (len(shapes) - out_far) + [hbm] * out_far,
        scratch_shapes=scratch,
        compiler_params=pltpu.CompilerParams(vmem_limit_bytes=16 * 1024 * 1024),
        cost_estimate=pl.CostEstimate(flops=0, bytes_accessed=1024, transcendentals=0),
    )(at, *scalars, *far, *args)


def product(kernel, at, args, scratch, rows=128, far=(), copies=0):
    work = 6 * 512 * 512 * 256
    return local(
        kernel, at, args, [(rows, 256)] * 4, scratch, copies=copies, far=far, flops=work
    )


def on_device(inv_local, coupling, tail_block, adjacency):
    xh, co, z, y, xl = (lax.axis_index(a) for a in AXES)
    x = 2 * xh + xl
    at = jnp.stack([x, y, z, co, xl, jnp.where(co == 0, y, z)]).astype(jnp.int32)
    along = {axis: functools.partial(partner, axis) for axis in "xyz"}
    piece, half_piece = (128, 256), (64, 256)
    wide, square = (512, 256), (512, 512)
    x8, y8 = ("xh", "xl", "co"), ("y", "co")

    factor, own, tail = coupling[0], inv_local[0], tail_block
    lane = jnp.where(co == 0, y, z)

    def dealt_for(r):
        def columns(a):
            v = lane ^ r
            starts = [jnp.where(co == 0, 512 * k + 128 * v, 512 * v + 128 * k) for k in range(4)]
            return jnp.concatenate([lax.dynamic_slice(a, (0, s), (64, 128)) for s in starts], axis=1)

        return jnp.stack([columns(factor), jnp.where(co == 0, columns(own), columns(tail))])

    count = adjacency.shape[0]
    joined = jnp.maximum(adjacency, jnp.eye(count, dtype=jnp.int32)).astype(jnp.float32)
    mask = lax.dynamic_index_in_dim(joined, (z * 8 + y * 2 + xl) * 64 // TILE, 0, keepdims=False)
    dealt = exchanged([dealt_for(r) for r in range(4)], deal)
    keep, give = local(
        pair_kernel, at, dealt + [factor, own], [(4, 5, 64, 256)] * 2, scalars=[mask]
    )
    got = send(give, to_other_core)
    *rows, t_all = local(
        row_kernel,
        at,
        [keep, got],
        [(n, 64, 256) for n in (4, 6, 4, 6)] + [(2, 64, 256)] * 4 + [(4, 64, 512)],
    )
    rows, rows_local = rows[:4], rows[4:]
    (uppers, mixed, lowers, *riders, t_one) = local(
        base_kernel,
        at,
        exchanged(rows, along["x"]),
        [(256, 256)] * 3 + [half_piece] * 4 + [(2, 64, 512)],
    )
    pieces = gathered(uppers, "y")
    lowers = gathered(lowers, "x")
    (t_aside,) = after([t_one], pieces[1])
    t_two = send(t_aside, to_other_core)
    pieces = list(after(pieces, tuple(lowers)))
    parts = product(
        cross_tail_kernel, at, [t_all, t_one, t_two] + pieces + riders, [wide, wide], 192
    )
    b_sib = send(jnp.stack([a[:128] for a in lowers]), to_other_core)
    rows_local = after(rows_local, parts[0])
    cross, columns = scattered(parts, "z")
    rows_local = exchanged(rows_local, along["x"])
    crosses, blocks = {3: cross}, {}
    (on_y,) = local(column_kernel, at, columns, [(256, 256)])

    for t in (3, 2, 1, 0):
        odd = t % 2 == 1
        first, second = ("y", "x") if odd else ("x", "y")
        if t < 3:
            mine = gathered(blocks[t + 1], second)
            if t == 2:
                (mixed,) = after([mixed], blocks[3])
                mixed = gathered(mixed, "x")
                x_own = jnp.concatenate(after(mine + [a_give], tuple(mixed)))
                (on_y,) = after([on_y], x_own)
                on_y = gathered(on_y, "y")
            else:
                x_own = jnp.concatenate(mine)
            args = [x_own, send(x_own, to_other_core)]
            if odd:
                args += pieces
            else:
                args += [a_own] if t else [a_own, b_sib]
            kernel = cross_odd_kernel if odd else cross_even_kernel
            parts = product(kernel, at, args, [wide, wide])
            cross, _ = scattered(parts, "z")
            crosses[t] = cross
        whole = gathered(cross, "z")
        if t == 2:
            on_y = list(after(on_y, tuple(whole)))
            on_y_sib = send(jnp.stack(on_y), to_other_core)
        args = list(lowers) + [b_sib] if odd else on_y + [on_y_sib]
        kernel = close_odd_kernel if odd else functools.partial(close_even_kernel, t // 2)
        args += whole
        parts = product(kernel, at, args, [square, wide, wide])
        if t == 3:
            rows_local = after(rows_local, parts[0])
            *locals_, a_own, a_give = local(
                local_kernel, at, list(rows_local) + lowers, [piece] * 4 + [(4, *half_piece), (256, 256)]
            )
        if t == 2:
            lowers = list(after(mixed, parts[0]))
            give, a_own = local(share_kernel, at, lowers, [(4, 192, 256), (4, *half_piece)])
            b_sib = send(give, to_other_core)
        blocks[t] = scattered(parts, first)[0] + locals_[t]

    outs = [a[t] for t in range(4) for a in (blocks, crosses)]
    outs = exchanged(local(leave_kernel, at, outs, [(2, 2, 64, 256)] * 4), along["x"])
    keep, give = local(meet_kernel, at, outs, [(4, 2, 64, 256)] * 2)
    got = send(give, to_other_core)
    turned = local(turn_kernel, at, [keep, got], [(2, 64, 512)] * 4)
    back = exchanged(turned, along["y"], lambda co, **_: co == 0)

    diag, off = local(
        finish_kernel, at, list(turned) + back[1:], [(64, 2048)] * 2, scalars=[mask]
    )
    return diag[None], off[None]


def solution(mesh):
    fine = Mesh(mesh.devices.reshape(SIZES), AXES)
    rows = P(("xh", "co"), ("z", "y", "xl"), None)
    return jax.shard_map(
        on_device,
        mesh=fine,
        in_specs=(rows, rows, P(("z", "y", "xl"), None), P()),
        out_specs=(rows, rows),
        check_vma=False,
    )
```

```python
import functools

import jax
import jax.numpy as jnp
import numpy as np
from jax import lax
from jax.experimental import pallas as pl
from jax.experimental.pallas import tpu as pltpu
from jax.sharding import Mesh, PartitionSpec as P

TILE = 128
AXES = ("xh", "co", "z", "y", "xl")
SIZES = (2, 2, 4, 4, 2)
X, Y, Z, C, XL, LANE = range(6)


def route(place, only=None):
    pairs = []
    for i in range(int(np.prod(SIZES))):
        xh, co, z, y, xl = (int(v) for v in np.unravel_index(i, SIZES))
        at = dict(x=2 * xh + xl, y=y, z=z, co=co)
        if only is not None and not only(**at):
            continue
        at = place(**at)
        to = (at["x"] // 2, at["co"], at["z"], at["y"], at["x"] % 2)
        pairs.append((i, int(np.ravel_multi_index(to, SIZES))))
    assert len({b for _, b in pairs}) == len(pairs)
    return pairs


def send(x, place, only=None):
    return lax.ppermute(x, AXES, route(place, only))


def partner(axis, r):
    def place(**at):
        return {**at, axis: at[axis] ^ r}

    return place


def deal(r):
    def place(**at):
        axis = "z" if at["co"] else "y"
        return {**at, axis: at[axis] ^ r}

    return place


def to_other_core(**at):
    return {**at, "co": 1 - at["co"]}


def exchanged(pieces, place, only=None):
    return [pieces[0]] + [send(pieces[r], place(r), only) for r in (1, 2, 3)]


def gathered(piece, axis):
    return exchanged([piece] * 4, functools.partial(partner, axis))


def scattered(parts, axis):
    got = exchanged(parts, functools.partial(partner, axis))
    return sum(a[:128] for a in got[1:]) + got[0][:128], got


def after(values, done):
    return lax.optimization_barrier((tuple(values), done))[0]


def split(x):
    hi = x.astype(jnp.bfloat16)
    lo = (x - hi.astype(jnp.float32)).astype(jnp.bfloat16)
    return hi, lo


def dot_cols(a, b):
    dims = (((0,), (0,)), ((), ()))
    mm = functools.partial(
        lax.dot_general, dimension_numbers=dims, preferred_element_type=jnp.float32
    )
    a_hi, a_lo = split(a)
    b_hi, b_lo = split(b)
    return mm(a_hi, b_hi) + (mm(a_hi, b_lo) + mm(a_lo, b_hi))


def dot_rows(a, b):
    mm = functools.partial(jnp.dot, preferred_element_type=jnp.float32)
    a_hi, a_lo = split(a)
    b_hi, b_lo = split(b)
    return mm(a_hi, b_hi) + (mm(a_hi, b_lo) + mm(a_lo, b_hi))


def rows_of(start, count):
    return pl.ds(pl.multiple_of(start, count), count)


def fetch(pairs, sems, first=0):
    copies = [
        pltpu.make_async_copy(a, b, sems.at[first + i]) for i, (a, b) in enumerate(pairs)
    ]
    for copy in copies:
        copy.start()
    return copies


def arrive(copies):
    for copy in copies:
        copy.wait()


def put_parts(value, place, outs):
    for r, o in enumerate(outs):
        o[pl.ds(0, 128), :] = value[rows_of(128 * (place ^ r), 128), :]


def put_pieces(pieces, place, ref):
    for r, piece in enumerate(pieces):
        ref[rows_of(128 * (place ^ r), 128), :] = piece[pl.ds(0, 128), :]


def cross_tail_kernel(at, t_own, t_one, t_two, *rest):
    pieces, riders, outs, (a, y) = rest[:4], rest[4:8], rest[8:12], rest[12:]
    for o, rider in zip(outs, riders):
        o[pl.ds(128, 64), :] = rider[...]
    put_pieces(pieces, at[Y], a)

    def put(ref, count, first, half):
        part = dot_rows(ref[...].reshape(count * 64, 512), a[...])
        for i in range(count):
            y[rows_of(128 * (first + i) + 64 * half, 64), :] = part[64 * i : 64 * i + 64]

    put(t_own, 4, 0, at[XL])
    put(t_one, 2, 2 * at[C], 1 - at[XL])
    put(t_two, 2, 2 * (1 - at[C]), 1 - at[XL])
    put_parts(y, at[Z], outs)


def cross_even_kernel(at, x_own, x_sib, a_own, *rest):
    o0, o1, o2, o3, a, y = rest[-6:]
    for r in range(4):
        row = 128 * (at[X] ^ at[Y] ^ r)
        theirs = rest[0][r, pl.ds(128, 64), :] if len(rest) > 6 else x_sib[pl.ds(512 + 64 * r, 64), :]
        a[rows_of(row + 64 * at[C], 64), :] = a_own[r]
        a[rows_of(row + 64 * (1 - at[C]), 64), :] = theirs
    cross_of(at, x_own, x_sib, a, y, (o0, o1, o2, o3))


def cross_odd_kernel(at, x_own, x_sib, a0, a1, a2, a3, o0, o1, o2, o3, a, y):
    for r, piece in enumerate((a0, a1, a2, a3)):
        a[rows_of(128 * (at[X] ^ at[Y] ^ r), 128), :] = piece[pl.ds(128, 128), :]
    cross_of(at, x_own, x_sib, a, y, (o0, o1, o2, o3))


def cross_of(at, x_own, x_sib, a, y, outs):
    for ref, half in ((x_own, at[C]), (x_sib, 1 - at[C])):
        y[rows_of(256 * half, 256), :] = dot_cols(ref[pl.ds(0, 512), :], a[...])
    put_parts(y, at[Z], outs)


def close_odd_kernel(at, b0, b1, b2, b3, b_sib, y0, y1, y2, y3, *rest):
    outs, (b, x, y) = rest[:4], rest[4:]
    put_pieces((y0, y1, y2, y3), at[Z], y)
    for r, own in enumerate((b0, b1, b2, b3)):
        rows = rows_of(128 * (at[X] ^ r), 128)
        b[rows, rows_of(256 * at[C], 256)] = own[pl.ds(0, 128), :]
        b[rows, rows_of(256 * (1 - at[C]), 256)] = b_sib[r, pl.ds(0, 128), :]
    x[...] = dot_cols(b[...], y[...])
    put_parts(x, at[Y], outs)


def close_even_kernel(slot, at, b0, b1, b2, b3, b_sib, y0, y1, y2, y3, *rest):
    outs, (b, x, y) = rest[:4], rest[4:]
    put_pieces((y0, y1, y2, y3), at[Z], y)
    here = pl.ds(128 * slot, 128)
    for r, own in enumerate((b0, b1, b2, b3)):
        cols = rows_of(128 * (at[Y] ^ r), 128)
        for k in range(4):
            b[rows_of(128 * k + 64 * at[C], 64), cols] = own[pl.ds(64 * k, 64), here]
            b[rows_of(128 * k + 64 * (1 - at[C]), 64), cols] = b_sib[r, pl.ds(64 * k, 64), here]
    x[...] = dot_cols(b[...], y[...])
    put_parts(x, at[X], outs)


def pair_kernel(at, mask, d0, d1, d2, d3, factor, local, keep, give):
    low, high = pl.ds(0, 256), pl.ds(256, 256)
    dealt = (d0, d1, d2, d3)

    def factors(ref):
        for r, d in enumerate(dealt):
            ref[at[LANE] ^ r, 0] = d[0, :, low]
            ref[at[LANE] ^ r, 1] = d[0, :, high]

    def nothing(ref, slots):
        for s in range(4):
            for k in slots:
                ref[s, k] = jnp.zeros((64, 256), jnp.float32)

    @pl.when(at[C] == 0)
    def _():
        for r, d in enumerate(dealt):
            keep[at[LANE] ^ r, 2] = d[1, :, low]
            give[at[LANE] ^ r, 2] = d[1, :, high]
        for ref in (keep, give):
            nothing(ref, (3, 4))

        @pl.when(at[XL] == 0)
        def _():
            factors(keep)
            nothing(give, (0, 1))

        @pl.when(at[XL] == 1)
        def _():
            factors(give)
            nothing(keep, (0, 1))

    @pl.when(at[C] == 1)
    def _():
        for r, d in enumerate(dealt):
            s = at[LANE] ^ r
            keep[s, 1] = d[0, :, high]
            give[s, 1] = d[0, :, low]
            for h, cols in enumerate((low, high)):
                keep[s, 3 + h] = d[1, :, cols]
                give[s, 3 + h] = d[1, :, cols]
        for s in range(4):
            for k, ref in ((0, factor), (2, local)):
                for i in range(2):
                    here = pl.ds(128 * i, 128)
                    give[s, k, :, here] = ref[:, pl.ds(512 * i + 128 * s, 128)]
                    keep[s, k, :, here] = ref[:, pl.ds(512 * (i + 2) + 128 * s, 128)]


def row_kernel(at, keep, got, *outs):
    rows, locals_, t_all = outs[:4], outs[4:8], outs[8]

    def fill(odd, even):
        for r, (a, e) in enumerate(zip(rows, locals_)):
            s = at[X] ^ r
            for k in range(2):
                a[k] = odd[s, k]
                a[2 + k] = even[s, k]
            e[0] = odd[s, 2]
            e[1] = even[s, 2]
        for s in range(4):
            for h in range(2):
                t_all[s, :, pl.ds(256 * h, 256)] = odd[s, 3 + h]
        for i, a in enumerate((rows[1], rows[3])):
            for h in range(2):
                a[4 + h] = odd[2 * at[C] + i, 3 + h]

    @pl.when(at[C] == 0)
    def _():
        fill(got, keep)

    @pl.when(at[C] == 1)
    def _():
        fill(keep, got)


def base_kernel(at, a0, a1, a2, a3, *outs):
    uppers, mixed, riders, t_one = outs[0], outs[1:3], outs[3:7], outs[7]
    for r, a in enumerate((a0, a1, a2, a3)):
        s = at[X] ^ r
        n = s // 2
        rows = rows_of(64 * lax.rem(s, 2), 64)
        for i in range(2):

            @pl.when(n == i)
            def _():
                uppers[rows_of(128 * (1 - i) + 64 * lax.rem(s, 2), 64), :] = a[0]
                mixed[i][rows, :] = a[1]

            @pl.when((n == i) & (lax.rem(s, 2) == at[C]))
            def _():
                for h in range(2):
                    mixed[i][pl.ds(128 + 64 * h, 64), :] = a[2 + h]

        @pl.when(lax.rem(s, 2) == at[C])
        def _():
            for k, rider in enumerate(riders):
                v = at[Z] ^ k
                block = a[2 + v // 2, :, rows_of(128 * lax.rem(v, 2), 128)]
                rider[:, rows_of(128 * n, 128)] = block

    for i, a in enumerate((a1, a3)):
        for h in range(2):
            t_one[i, :, pl.ds(256 * h, 256)] = a[4 + h]


def share_kernel(at, a0, a1, a2, a3, give, a_own):
    for r, a in enumerate((a0, a1, a2, a3)):
        give[r, pl.ds(0, 128), :] = a[pl.ds(0, 128), :]
        give[r, pl.ds(128, 64), :] = a[rows_of(128 + 64 * (1 - at[C]), 64), :]
        a_own[r] = a[rows_of(128 + 64 * at[C], 64), :]


def column_kernel(at, e0, e1, e2, e3, out):
    for r, e in enumerate((e0, e1, e2, e3)):
        out[rows_of(64 * (at[Z] ^ r), 64), :] = e[pl.ds(128, 64), :]


def local_kernel(at, e0, e1, e2, e3, m0, m1, m2, m3, *outs):
    a_own, a_give = outs[4:]
    for r, m in enumerate((m0, m1, m2, m3)):
        a_own[r] = m[rows_of(128 + 64 * at[C], 64), :]
        a_give[pl.ds(64 * r, 64), :] = m[rows_of(128 + 64 * (1 - at[C]), 64), :]
    for r, e in enumerate((e0, e1, e2, e3)):
        s = at[X] ^ r
        for n in range(2):

            @pl.when(s // 2 == n)
            def _():
                rows = rows_of(64 * lax.rem(s, 2), 64)
                outs[2 * n][rows, :] = e[1]
                outs[2 * n + 1][rows, :] = e[0]


def leave_kernel(at, *refs):
    kept, outs = refs[:8], refs[8:]
    for r, out in enumerate(outs):
        for s in range(4):

            @pl.when((at[X] ^ r) == s)
            def _():
                for n in range(2):
                    for k in range(2):
                        ref = kept[2 * (2 * (s // 2) + n) + k]
                        out[n, k] = ref[pl.ds(64 * (s % 2), 64), :]


def meet_kernel(at, a0, a1, a2, a3, *outs):
    rest = outs[4]
    for k, a in enumerate((a0, a1, a2, a3)):
        rest[at[X] ^ k] = a[1]
        for r in range(4):

            @pl.when((at[X] ^ at[Y] ^ k) == r)
            def _():
                outs[r][...] = a[0]


def turn_kernel(at, h0, h1, h2, h3, rest, keep, give):
    @pl.when(at[C] == 0)
    def _():
        for r, h in enumerate((h0, h1, h2, h3)):
            keep[at[Y] ^ r] = h[...]
        give[...] = rest[...]

    @pl.when(at[C] == 1)
    def _():
        for r, h in enumerate((h0, h1, h2, h3)):
            give[at[Y] ^ r] = h[...]
        keep[...] = rest[...]


def finish_kernel(at, mask, keep, got, diag, off):
    for ref, half in ((keep, at[C]), (got, 1 - at[C])):
        for s in range(4):
            for i in range(2):
                block = 4 * (2 * half + i) + s
                cols = rows_of(128 * block, 128)
                kept = mask[block]
                diag[:, cols] = ref[s, 0, :, pl.ds(128 * i, 128)] * kept
                off[:, cols] = -ref[s, 1, :, pl.ds(128 * i, 128)] * kept


def local(kernel, at, args, shapes, scratch=(), copies=0, scalars=(), far=(), flops=0, out_far=0):
    vmem = pl.BlockSpec(memory_space=pltpu.VMEM)
    smem = pl.BlockSpec(memory_space=pltpu.SMEM)
    hbm = pl.BlockSpec(memory_space=pltpu.HBM)
    moved = sum(int(np.prod(a.shape)) for a in args) + sum(int(np.prod(s)) for s in shapes)
    scratch = [pltpu.VMEM(s, jnp.float32) for s in scratch]
    if copies:
        scratch.append(pltpu.SemaphoreType.DMA((copies,)))
    return pl.pallas_call(
        kernel,
        out_shape=[jax.ShapeDtypeStruct(s, jnp.float32) for s in shapes],
        in_specs=[smem] * (1 + len(scalars)) + [hbm] * len(far) + [vmem] * len(args),
        out_specs=[vmem] * (len(shapes) - out_far) + [hbm] * out_far,
        scratch_shapes=scratch,
        compiler_params=pltpu.CompilerParams(vmem_limit_bytes=16 * 1024 * 1024),
        cost_estimate=pl.CostEstimate(flops=0, bytes_accessed=1024, transcendentals=0),
    )(at, *scalars, *far, *args)


def product(kernel, at, args, scratch, rows=128, far=(), copies=0):
    work = 6 * 512 * 512 * 256
    return local(
        kernel, at, args, [(rows, 256)] * 4, scratch, copies=copies, far=far, flops=work
    )


def on_device(inv_local, coupling, tail_block, adjacency):
    xh, co, z, y, xl = (lax.axis_index(a) for a in AXES)
    x = 2 * xh + xl
    at = jnp.stack([x, y, z, co, xl, jnp.where(co == 0, y, z)]).astype(jnp.int32)
    along = {axis: functools.partial(partner, axis) for axis in "xyz"}
    piece, half_piece = (128, 256), (64, 256)
    wide, square = (512, 256), (512, 512)
    x8, y8 = ("xh", "xl", "co"), ("y", "co")

    factor, own, tail = coupling[0], inv_local[0], tail_block
    lane = jnp.where(co == 0, y, z)

    def dealt_for(r):
        def columns(a):
            v = lane ^ r
            starts = [jnp.where(co == 0, 512 * k + 128 * v, 512 * v + 128 * k) for k in range(4)]
            return jnp.concatenate([lax.dynamic_slice(a, (0, s), (64, 128)) for s in starts], axis=1)

        return jnp.stack([columns(factor), jnp.where(co == 0, columns(own), columns(tail))])

    count = adjacency.shape[0]
    joined = jnp.maximum(adjacency, jnp.eye(count, dtype=jnp.int32)).astype(jnp.float32)
    mask = lax.dynamic_index_in_dim(joined, (z * 8 + y * 2 + xl) * 64 // TILE, 0, keepdims=False)
    dealt = exchanged([dealt_for(r) for r in range(4)], deal)
    keep, give = local(
        pair_kernel, at, dealt + [factor, own], [(4, 5, 64, 256)] * 2, scalars=[mask]
    )
    got = send(give, to_other_core)
    *rows, t_all = local(
        row_kernel,
        at,
        [keep, got],
        [(n, 64, 256) for n in (4, 6, 4, 6)] + [(2, 64, 256)] * 4 + [(4, 64, 512)],
    )
    rows, rows_local = rows[:4], rows[4:]
    (uppers, mixed, lowers, *riders, t_one) = local(
        base_kernel,
        at,
        exchanged(rows, along["x"]),
        [(256, 256)] * 3 + [half_piece] * 4 + [(2, 64, 512)],
    )
    pieces = gathered(uppers, "y")
    lowers = gathered(lowers, "x")
    (t_aside,) = after([t_one], pieces[1])
    t_two = send(t_aside, to_other_core)
    pieces = list(after(pieces, tuple(lowers)))
    parts = product(
        cross_tail_kernel, at, [t_all, t_one, t_two] + pieces + riders, [wide, wide], 192
    )
    b_sib = send(jnp.stack([a[:128] for a in lowers]), to_other_core)
    rows_local = after(rows_local, parts[0])
    cross, columns = scattered(parts, "z")
    rows_local = exchanged(rows_local, along["x"])
    crosses, blocks = {3: cross}, {}
    (on_y,) = local(column_kernel, at, columns, [(256, 256)])

    for t in (3, 2, 1, 0):
        odd = t % 2 == 1
        first, second = ("y", "x") if odd else ("x", "y")
        if t < 3:
            mine = gathered(blocks[t + 1], second)
            if t == 2:
                (mixed,) = after([mixed], blocks[3])
                mixed = gathered(mixed, "x")
                x_own = jnp.concatenate(after(mine + [a_give], tuple(mixed)))
                (on_y,) = after([on_y], x_own)
                on_y = gathered(on_y, "y")
            else:
                x_own = jnp.concatenate(mine)
            args = [x_own, send(x_own, to_other_core)]
            if odd:
                args += pieces
            else:
                args += [a_own] if t else [a_own, b_sib]
            kernel = cross_odd_kernel if odd else cross_even_kernel
            parts = product(kernel, at, args, [wide, wide])
            cross, _ = scattered(parts, "z")
            crosses[t] = cross
        whole = gathered(cross, "z")
        if t == 2:
            on_y = list(after(on_y, tuple(whole)))
            on_y_sib = send(jnp.stack(on_y), to_other_core)
        args = list(lowers) + [b_sib] if odd else on_y + [on_y_sib]
        kernel = close_odd_kernel if odd else functools.partial(close_even_kernel, t // 2)
        args += whole
        parts = product(kernel, at, args, [square, wide, wide])
        if t == 3:
            rows_local = after(rows_local, parts[0])
            *locals_, a_own, a_give = local(
                local_kernel, at, list(rows_local) + lowers, [piece] * 4 + [(4, *half_piece), (256, 256)]
            )
        if t == 2:
            lowers = list(after(mixed, parts[0]))
            give, a_own = local(share_kernel, at, lowers, [(4, 192, 256), (4, *half_piece)])
            b_sib = send(give, to_other_core)
        blocks[t] = scattered(parts, first)[0] + locals_[t]

    outs = [a[t] for t in range(4) for a in (blocks, crosses)]
    outs = exchanged(local(leave_kernel, at, outs, [(2, 2, 64, 256)] * 4), along["x"])
    *turned, rest = local(meet_kernel, at, outs, [(2, 64, 256)] * 4 + [(4, 2, 64, 256)])
    turned = exchanged(turned, along["y"])
    keep, give = local(turn_kernel, at, turned + [rest], [(4, 2, 64, 256)] * 2)
    got = send(give, to_other_core)
    diag, off = local(finish_kernel, at, [keep, got], [(64, 2048)] * 2, scalars=[mask])
    return diag[None], off[None]


def solution(mesh):
    fine = Mesh(mesh.devices.reshape(SIZES), AXES)
    rows = P(("xh", "co"), ("z", "y", "xl"), None)
    return jax.shard_map(
        on_device,
        mesh=fine,
        in_specs=(rows, rows, P(("z", "y", "xl"), None), P()),
        out_specs=(rows, rows),
        check_vma=False,
    )
```

```python
import functools

import jax
import jax.numpy as jnp
import numpy as np
from jax import lax
from jax.experimental import pallas as pl
from jax.experimental.pallas import tpu as pltpu
from jax.sharding import Mesh, PartitionSpec as P

TILE = 128
AXES = ("xh", "co", "z", "y", "xl")
SIZES = (2, 2, 4, 4, 2)
X, Y, Z, C, XL, LANE = range(6)


def route(place, only=None):
    pairs = []
    for i in range(int(np.prod(SIZES))):
        xh, co, z, y, xl = (int(v) for v in np.unravel_index(i, SIZES))
        at = dict(x=2 * xh + xl, y=y, z=z, co=co)
        if only is not None and not only(**at):
            continue
        at = place(**at)
        to = (at["x"] // 2, at["co"], at["z"], at["y"], at["x"] % 2)
        pairs.append((i, int(np.ravel_multi_index(to, SIZES))))
    assert len({b for _, b in pairs}) == len(pairs)
    return pairs


def send(x, place, only=None):
    return lax.ppermute(x, AXES, route(place, only))


def partner(axis, r):
    def place(**at):
        return {**at, axis: at[axis] ^ r}

    return place


def deal(r):
    def place(**at):
        axis = "z" if at["co"] else "y"
        return {**at, axis: at[axis] ^ r}

    return place


def to_other_core(**at):
    return {**at, "co": 1 - at["co"]}


def exchanged(pieces, place, only=None):
    return [pieces[0]] + [send(pieces[r], place(r), only) for r in (1, 2, 3)]


def gathered(piece, axis):
    return exchanged([piece] * 4, functools.partial(partner, axis))


def scattered(parts, axis):
    got = exchanged(parts, functools.partial(partner, axis))
    return sum(a[:128] for a in got[1:]) + got[0][:128], got


def after(values, done):
    return lax.optimization_barrier((tuple(values), done))[0]


def split(x):
    hi = x.astype(jnp.bfloat16)
    lo = (x - hi.astype(jnp.float32)).astype(jnp.bfloat16)
    return hi, lo


def dot_cols(a, b):
    dims = (((0,), (0,)), ((), ()))
    mm = functools.partial(
        lax.dot_general, dimension_numbers=dims, preferred_element_type=jnp.float32
    )
    a_hi, a_lo = split(a)
    b_hi, b_lo = split(b)
    return mm(a_hi, b_hi) + (mm(a_hi, b_lo) + mm(a_lo, b_hi))


def dot_rows(a, b):
    mm = functools.partial(jnp.dot, preferred_element_type=jnp.float32)
    a_hi, a_lo = split(a)
    b_hi, b_lo = split(b)
    return mm(a_hi, b_hi) + (mm(a_hi, b_lo) + mm(a_lo, b_hi))


def rows_of(start, count):
    return pl.ds(pl.multiple_of(start, count), count)


def fetch(pairs, sems, first=0):
    copies = [
        pltpu.make_async_copy(a, b, sems.at[first + i]) for i, (a, b) in enumerate(pairs)
    ]
    for copy in copies:
        copy.start()
    return copies


def arrive(copies):
    for copy in copies:
        copy.wait()


def put_parts(value, place, outs):
    for r, o in enumerate(outs):
        o[pl.ds(0, 128), :] = value[rows_of(128 * (place ^ r), 128), :]


def put_pieces(pieces, place, ref):
    for r, piece in enumerate(pieces):
        ref[rows_of(128 * (place ^ r), 128), :] = piece[pl.ds(0, 128), :]


def cross_tail_kernel(at, t_own, t_one, t_two, *rest):
    pieces, riders, outs, (a, y) = rest[:4], rest[4:8], rest[8:12], rest[12:]
    for o, rider in zip(outs, riders):
        o[pl.ds(128, 64), :] = rider[...]
    put_pieces(pieces, at[Y], a)

    def put(ref, count, first, half):
        part = dot_rows(ref[...].reshape(count * 64, 512), a[...])
        for i in range(count):
            y[rows_of(128 * (first + i) + 64 * half, 64), :] = part[64 * i : 64 * i + 64]

    put(t_own, 4, 0, at[XL])
    put(t_one, 2, 2 * at[C], 1 - at[XL])
    put(t_two, 2, 2 * (1 - at[C]), 1 - at[XL])
    put_parts(y, at[Z], outs)


def cross_even_kernel(at, x_own, x_sib, a_own, *rest):
    o0, o1, o2, o3, a, y = rest[-6:]
    for r in range(4):
        row = 128 * (at[X] ^ at[Y] ^ r)
        theirs = rest[0][r, pl.ds(128, 64), :] if len(rest) > 6 else x_sib[pl.ds(512 + 64 * r, 64), :]
        a[rows_of(row + 64 * at[C], 64), :] = a_own[r]
        a[rows_of(row + 64 * (1 - at[C]), 64), :] = theirs
    cross_of(at, x_own, x_sib, a, y, (o0, o1, o2, o3))


def cross_odd_kernel(at, x_own, x_sib, a0, a1, a2, a3, o0, o1, o2, o3, a, y):
    for r, piece in enumerate((a0, a1, a2, a3)):
        a[rows_of(128 * (at[X] ^ at[Y] ^ r), 128), :] = piece[pl.ds(128, 128), :]
    cross_of(at, x_own, x_sib, a, y, (o0, o1, o2, o3))


def cross_of(at, x_own, x_sib, a, y, outs):
    for ref, half in ((x_own, at[C]), (x_sib, 1 - at[C])):
        y[rows_of(256 * half, 256), :] = dot_cols(ref[pl.ds(0, 512), :], a[...])
    put_parts(y, at[Z], outs)


def close_odd_kernel(at, b0, b1, b2, b3, b_sib, y0, y1, y2, y3, *rest):
    outs, (b, x, y) = rest[:4], rest[4:]
    put_pieces((y0, y1, y2, y3), at[Z], y)
    for r, own in enumerate((b0, b1, b2, b3)):
        rows = rows_of(128 * (at[X] ^ r), 128)
        b[rows, rows_of(256 * at[C], 256)] = own[pl.ds(0, 128), :]
        b[rows, rows_of(256 * (1 - at[C]), 256)] = b_sib[r, pl.ds(0, 128), :]
    x[...] = dot_cols(b[...], y[...])
    put_parts(x, at[Y], outs)


def close_even_kernel(slot, at, b0, b1, b2, b3, b_sib, y0, y1, y2, y3, *rest):
    outs, (b, x, y) = rest[:4], rest[4:]
    put_pieces((y0, y1, y2, y3), at[Z], y)
    here = pl.ds(128 * slot, 128)
    for r, own in enumerate((b0, b1, b2, b3)):
        cols = rows_of(128 * (at[Y] ^ r), 128)
        for k in range(4):
            b[rows_of(128 * k + 64 * at[C], 64), cols] = own[pl.ds(64 * k, 64), here]
            b[rows_of(128 * k + 64 * (1 - at[C]), 64), cols] = b_sib[r, pl.ds(64 * k, 64), here]
    x[...] = dot_cols(b[...], y[...])
    put_parts(x, at[X], outs)


def pair_kernel(at, mask, d0, d1, d2, d3, factor, local, keep, give):
    low, high = pl.ds(0, 256), pl.ds(256, 256)
    dealt = (d0, d1, d2, d3)

    def factors(ref):
        for r, d in enumerate(dealt):
            ref[at[LANE] ^ r, 0] = d[0, :, low]
            ref[at[LANE] ^ r, 1] = d[0, :, high]

    def nothing(ref, slots):
        for s in range(4):
            for k in slots:
                ref[s, k] = jnp.zeros((64, 256), jnp.float32)

    @pl.when(at[C] == 0)
    def _():
        for r, d in enumerate(dealt):
            keep[at[LANE] ^ r, 2] = d[1, :, low]
            give[at[LANE] ^ r, 2] = d[1, :, high]
        for ref in (keep, give):
            nothing(ref, (3, 4))

        @pl.when(at[XL] == 0)
        def _():
            factors(keep)
            nothing(give, (0, 1))

        @pl.when(at[XL] == 1)
        def _():
            factors(give)
            nothing(keep, (0, 1))

    @pl.when(at[C] == 1)
    def _():
        for r, d in enumerate(dealt):
            s = at[LANE] ^ r
            keep[s, 1] = d[0, :, high]
            give[s, 1] = d[0, :, low]
            for h, cols in enumerate((low, high)):
                keep[s, 3 + h] = d[1, :, cols]
                give[s, 3 + h] = d[1, :, cols]
        for s in range(4):
            for k, ref in ((0, factor), (2, local)):
                for i in range(2):
                    here = pl.ds(128 * i, 128)
                    give[s, k, :, here] = ref[:, pl.ds(512 * i + 128 * s, 128)]
                    keep[s, k, :, here] = ref[:, pl.ds(512 * (i + 2) + 128 * s, 128)]


def row_kernel(at, keep, got, *outs):
    rows, locals_, t_all = outs[:4], outs[4:8], outs[8]

    def fill(odd, even):
        for r, (a, e) in enumerate(zip(rows, locals_)):
            s = at[X] ^ r
            for k in range(2):
                a[k] = odd[s, k]
                a[2 + k] = even[s, k]
            e[0] = odd[s, 2]
            e[1] = even[s, 2]
        for s in range(4):
            for h in range(2):
                t_all[s, :, pl.ds(256 * h, 256)] = odd[s, 3 + h]
        for i, a in enumerate((rows[1], rows[3])):
            for h in range(2):
                a[4 + h] = odd[2 * at[C] + i, 3 + h]

    @pl.when(at[C] == 0)
    def _():
        fill(got, keep)

    @pl.when(at[C] == 1)
    def _():
        fill(keep, got)


def base_kernel(at, a0, a1, a2, a3, *outs):
    uppers, mixed, riders, t_one = outs[0], outs[1:3], outs[3:7], outs[7]
    for r, a in enumerate((a0, a1, a2, a3)):
        s = at[X] ^ r
        n = s // 2
        rows = rows_of(64 * lax.rem(s, 2), 64)
        for i in range(2):

            @pl.when(n == i)
            def _():
                uppers[rows_of(128 * (1 - i) + 64 * lax.rem(s, 2), 64), :] = a[0]
                mixed[i][rows, :] = a[1]

            @pl.when((n == i) & (lax.rem(s, 2) == at[C]))
            def _():
                for h in range(2):
                    mixed[i][pl.ds(128 + 64 * h, 64), :] = a[2 + h]

        @pl.when(lax.rem(s, 2) == at[C])
        def _():
            for k, rider in enumerate(riders):
                v = at[Z] ^ k
                block = a[2 + v // 2, :, rows_of(128 * lax.rem(v, 2), 128)]
                rider[:, rows_of(128 * n, 128)] = block

    for i, a in enumerate((a1, a3)):
        for h in range(2):
            t_one[i, :, pl.ds(256 * h, 256)] = a[4 + h]


def share_kernel(at, a0, a1, a2, a3, give, a_own):
    for r, a in enumerate((a0, a1, a2, a3)):
        give[r, pl.ds(0, 128), :] = a[pl.ds(0, 128), :]
        give[r, pl.ds(128, 64), :] = a[rows_of(128 + 64 * (1 - at[C]), 64), :]
        a_own[r] = a[rows_of(128 + 64 * at[C], 64), :]


def column_kernel(at, e0, e1, e2, e3, out):
    for r, e in enumerate((e0, e1, e2, e3)):
        out[rows_of(64 * (at[Z] ^ r), 64), :] = e[pl.ds(128, 64), :]


def local_kernel(at, e0, e1, e2, e3, m0, m1, m2, m3, *outs):
    a_own, a_give = outs[4:]
    for r, m in enumerate((m0, m1, m2, m3)):
        a_own[r] = m[rows_of(128 + 64 * at[C], 64), :]
        a_give[pl.ds(64 * r, 64), :] = m[rows_of(128 + 64 * (1 - at[C]), 64), :]
    for r, e in enumerate((e0, e1, e2, e3)):
        s = at[X] ^ r
        for n in range(2):

            @pl.when(s // 2 == n)
            def _():
                rows = rows_of(64 * lax.rem(s, 2), 64)
                outs[2 * n][rows, :] = e[1]
                outs[2 * n + 1][rows, :] = e[0]


def early_kernel(at, x1, y1, x2, y2, x3, y3, *outs):
    for r, out in enumerate(outs):
        for s in range(4):

            @pl.when((at[X] ^ r) == s)
            def _():
                rows = pl.ds(64 * (s % 2), 64)
                steps = ((x2, y2), (x3, y3)) if s // 2 else ((x1, y1), (x1, y1))
                for n, step in enumerate(steps):
                    for k, ref in enumerate(step):
                        out[n, k] = ref[rows, :]


def late_kernel(at, x0, y0, *outs):
    for r, out in enumerate(outs):
        rows = rows_of(64 * lax.rem(at[X] ^ r, 2), 64)
        out[0] = x0[rows, :]
        out[1] = y0[rows, :]


def meet_kernel(at, e0, e1, e2, e3, l0, l1, l2, l3, *outs):
    rest = outs[4]
    for k, (early, late) in enumerate(((e0, l0), (e1, l1), (e2, l2), (e3, l3))):
        rest[at[X] ^ k] = early[1]
        for r in range(4):
            here = (at[X] ^ at[Y] ^ k) == r

            @pl.when(here & (at[X] // 2 == 0))
            def _():
                outs[r][...] = late[...]

            @pl.when(here & (at[X] // 2 == 1))
            def _():
                outs[r][...] = early[0]


def turn_kernel(at, h0, h1, h2, h3, rest, keep, give):
    @pl.when(at[C] == 0)
    def _():
        for r, h in enumerate((h0, h1, h2, h3)):
            keep[at[Y] ^ r] = h[...]
        give[...] = rest[...]

    @pl.when(at[C] == 1)
    def _():
        for r, h in enumerate((h0, h1, h2, h3)):
            give[at[Y] ^ r] = h[...]
        keep[...] = rest[...]


def finish_kernel(at, mask, keep, got, diag, off):
    for ref, half in ((keep, at[C]), (got, 1 - at[C])):
        for s in range(4):
            for i in range(2):
                block = 4 * (2 * half + i) + s
                cols = rows_of(128 * block, 128)
                kept = mask[block]
                diag[:, cols] = ref[s, 0, :, pl.ds(128 * i, 128)] * kept
                off[:, cols] = -ref[s, 1, :, pl.ds(128 * i, 128)] * kept


def local(kernel, at, args, shapes, scratch=(), copies=0, scalars=(), far=(), flops=0, out_far=0):
    vmem = pl.BlockSpec(memory_space=pltpu.VMEM)
    smem = pl.BlockSpec(memory_space=pltpu.SMEM)
    hbm = pl.BlockSpec(memory_space=pltpu.HBM)
    moved = sum(int(np.prod(a.shape)) for a in args) + sum(int(np.prod(s)) for s in shapes)
    scratch = [pltpu.VMEM(s, jnp.float32) for s in scratch]
    if copies:
        scratch.append(pltpu.SemaphoreType.DMA((copies,)))
    return pl.pallas_call(
        kernel,
        out_shape=[jax.ShapeDtypeStruct(s, jnp.float32) for s in shapes],
        in_specs=[smem] * (1 + len(scalars)) + [hbm] * len(far) + [vmem] * len(args),
        out_specs=[vmem] * (len(shapes) - out_far) + [hbm] * out_far,
        scratch_shapes=scratch,
        compiler_params=pltpu.CompilerParams(vmem_limit_bytes=16 * 1024 * 1024),
        cost_estimate=pl.CostEstimate(flops=0, bytes_accessed=1024, transcendentals=0),
    )(at, *scalars, *far, *args)


def product(kernel, at, args, scratch, rows=128, far=(), copies=0):
    work = 6 * 512 * 512 * 256
    return local(
        kernel, at, args, [(rows, 256)] * 4, scratch, copies=copies, far=far, flops=work
    )


def on_device(inv_local, coupling, tail_block, adjacency):
    xh, co, z, y, xl = (lax.axis_index(a) for a in AXES)
    x = 2 * xh + xl
    at = jnp.stack([x, y, z, co, xl, jnp.where(co == 0, y, z)]).astype(jnp.int32)
    along = {axis: functools.partial(partner, axis) for axis in "xyz"}
    piece, half_piece = (128, 256), (64, 256)
    wide, square = (512, 256), (512, 512)
    x8, y8 = ("xh", "xl", "co"), ("y", "co")

    factor, own, tail = coupling[0], inv_local[0], tail_block
    lane = jnp.where(co == 0, y, z)

    def dealt_for(r):
        def columns(a):
            v = lane ^ r
            starts = [jnp.where(co == 0, 512 * k + 128 * v, 512 * v + 128 * k) for k in range(4)]
            return jnp.concatenate([lax.dynamic_slice(a, (0, s), (64, 128)) for s in starts], axis=1)

        return jnp.stack([columns(factor), jnp.where(co == 0, columns(own), columns(tail))])

    count = adjacency.shape[0]
    joined = jnp.maximum(adjacency, jnp.eye(count, dtype=jnp.int32)).astype(jnp.float32)
    mask = lax.dynamic_index_in_dim(joined, (z * 8 + y * 2 + xl) * 64 // TILE, 0, keepdims=False)
    dealt = exchanged([dealt_for(r) for r in range(4)], deal)
    keep, give = local(
        pair_kernel, at, dealt + [factor, own], [(4, 5, 64, 256)] * 2, scalars=[mask]
    )
    got = send(give, to_other_core)
    *rows, t_all = local(
        row_kernel,
        at,
        [keep, got],
        [(n, 64, 256) for n in (4, 6, 4, 6)] + [(2, 64, 256)] * 4 + [(4, 64, 512)],
    )
    rows, rows_local = rows[:4], rows[4:]
    (uppers, mixed, lowers, *riders, t_one) = local(
        base_kernel,
        at,
        exchanged(rows, along["x"]),
        [(256, 256)] * 3 + [half_piece] * 4 + [(2, 64, 512)],
    )
    pieces = gathered(uppers, "y")
    lowers = gathered(lowers, "x")
    (t_aside,) = after([t_one], pieces[1])
    t_two = send(t_aside, to_other_core)
    pieces = list(after(pieces, tuple(lowers)))
    parts = product(
        cross_tail_kernel, at, [t_all, t_one, t_two] + pieces + riders, [wide, wide], 192
    )
    b_sib = send(jnp.stack([a[:128] for a in lowers]), to_other_core)
    rows_local = after(rows_local, parts[0])
    cross, columns = scattered(parts, "z")
    rows_local = exchanged(rows_local, along["x"])
    crosses, blocks = {3: cross}, {}
    (on_y,) = local(column_kernel, at, columns, [(256, 256)])

    for t in (3, 2, 1, 0):
        odd = t % 2 == 1
        first, second = ("y", "x") if odd else ("x", "y")
        if t == 0:
            early = [a[s] for s in (1, 2, 3) for a in (blocks, crosses)]
            early = local(early_kernel, at, early, [(2, 2, 64, 256)] * 4)
            early = exchanged(early, along["x"])
        if t < 3:
            mine = gathered(blocks[t + 1], second)
            if t == 2:
                (mixed,) = after([mixed], blocks[3])
                mixed = gathered(mixed, "x")
                x_own = jnp.concatenate(after(mine + [a_give], tuple(mixed)))
                (on_y,) = after([on_y], x_own)
                on_y = gathered(on_y, "y")
            else:
                x_own = jnp.concatenate(mine)
            args = [x_own, send(x_own, to_other_core)]
            if odd:
                args += pieces
            else:
                args += [a_own] if t else [a_own, b_sib]
            kernel = cross_odd_kernel if odd else cross_even_kernel
            parts = product(kernel, at, args, [wide, wide])
            cross, _ = scattered(parts, "z")
            crosses[t] = cross
        whole = gathered(cross, "z")
        if t == 0:
            whole = list(after(whole, tuple(early)))
        if t == 2:
            on_y = list(after(on_y, tuple(whole)))
            on_y_sib = send(jnp.stack(on_y), to_other_core)
        args = list(lowers) + [b_sib] if odd else on_y + [on_y_sib]
        kernel = close_odd_kernel if odd else functools.partial(close_even_kernel, t // 2)
        args += whole
        parts = product(kernel, at, args, [square, wide, wide])
        if t == 3:
            rows_local = after(rows_local, parts[0])
            *locals_, a_own, a_give = local(
                local_kernel, at, list(rows_local) + lowers, [piece] * 4 + [(4, *half_piece), (256, 256)]
            )
        if t == 2:
            lowers = list(after(mixed, parts[0]))
            give, a_own = local(share_kernel, at, lowers, [(4, 192, 256), (4, *half_piece)])
            b_sib = send(give, to_other_core)
        blocks[t] = scattered(parts, first)[0] + locals_[t]

    late = local(late_kernel, at, [blocks[0], crosses[0]], [(2, 64, 256)] * 4)
    late = [late[0]] + [
        send(late[r], along["x"](r), lambda x, **_: (x ^ r) // 2 == 0) for r in (1, 2, 3)
    ]
    *turned, rest = local(
        meet_kernel, at, early + late, [(2, 64, 256)] * 4 + [(4, 2, 64, 256)]
    )
    turned = exchanged(turned, along["y"])
    keep, give = local(turn_kernel, at, turned + [rest], [(4, 2, 64, 256)] * 2)
    got = send(give, to_other_core)
    diag, off = local(finish_kernel, at, [keep, got], [(64, 2048)] * 2, scalars=[mask])
    return diag[None], off[None]


def solution(mesh):
    fine = Mesh(mesh.devices.reshape(SIZES), AXES)
    rows = P(("xh", "co"), ("z", "y", "xl"), None)
    return jax.shard_map(
        on_device,
        mesh=fine,
        in_specs=(rows, rows, P(("z", "y", "xl"), None), P()),
        out_specs=(rows, rows),
        check_vma=False,
    )
```

```python
import functools

import jax
import jax.numpy as jnp
import numpy as np
from jax import lax
from jax.experimental import pallas as pl
from jax.experimental.pallas import tpu as pltpu
from jax.sharding import Mesh, PartitionSpec as P

TILE = 128
AXES = ("xh", "co", "z", "y", "xl")
SIZES = (2, 2, 4, 4, 2)
X, Y, Z, C, XL, LANE = range(6)


def route(place, only=None):
    pairs = []
    for i in range(int(np.prod(SIZES))):
        xh, co, z, y, xl = (int(v) for v in np.unravel_index(i, SIZES))
        at = dict(x=2 * xh + xl, y=y, z=z, co=co)
        if only is not None and not only(**at):
            continue
        at = place(**at)
        to = (at["x"] // 2, at["co"], at["z"], at["y"], at["x"] % 2)
        pairs.append((i, int(np.ravel_multi_index(to, SIZES))))
    assert len({b for _, b in pairs}) == len(pairs)
    return pairs


def send(x, place, only=None):
    return lax.ppermute(x, AXES, route(place, only))


def partner(axis, r):
    def place(**at):
        return {**at, axis: at[axis] ^ r}

    return place


def deal(r):
    def place(**at):
        axis = "z" if at["co"] else "y"
        return {**at, axis: at[axis] ^ r}

    return place


def to_other_core(**at):
    return {**at, "co": 1 - at["co"]}


def exchanged(pieces, place, only=None):
    return [pieces[0]] + [send(pieces[r], place(r), only) for r in (1, 2, 3)]


def gathered(piece, axis):
    return exchanged([piece] * 4, functools.partial(partner, axis))


def scattered(parts, axis):
    got = exchanged(parts, functools.partial(partner, axis))
    return sum(a[:128] for a in got[1:]) + got[0][:128], got


def after(values, done):
    return lax.optimization_barrier((tuple(values), done))[0]


def split(x):
    hi = x.astype(jnp.bfloat16)
    lo = (x - hi.astype(jnp.float32)).astype(jnp.bfloat16)
    return hi, lo


def dot_cols(a, b):
    dims = (((0,), (0,)), ((), ()))
    mm = functools.partial(
        lax.dot_general, dimension_numbers=dims, preferred_element_type=jnp.float32
    )
    a_hi, a_lo = split(a)
    b_hi, b_lo = split(b)
    return mm(a_hi, b_hi) + (mm(a_hi, b_lo) + mm(a_lo, b_hi))


def dot_rows(a, b):
    mm = functools.partial(jnp.dot, preferred_element_type=jnp.float32)
    a_hi, a_lo = split(a)
    b_hi, b_lo = split(b)
    return mm(a_hi, b_hi) + (mm(a_hi, b_lo) + mm(a_lo, b_hi))


def rows_of(start, count):
    return pl.ds(pl.multiple_of(start, count), count)


def fetch(pairs, sems, first=0):
    copies = [
        pltpu.make_async_copy(a, b, sems.at[first + i]) for i, (a, b) in enumerate(pairs)
    ]
    for copy in copies:
        copy.start()
    return copies


def arrive(copies):
    for copy in copies:
        copy.wait()


def put_parts(value, place, outs):
    for r, o in enumerate(outs):
        o[pl.ds(0, 128), :] = value[rows_of(128 * (place ^ r), 128), :]


def put_pieces(pieces, place, ref):
    for r, piece in enumerate(pieces):
        ref[rows_of(128 * (place ^ r), 128), :] = piece[pl.ds(0, 128), :]


def cross_tail_kernel(at, t_own, t_one, t_two, *rest):
    pieces, riders, outs, (a, y) = rest[:4], rest[4:8], rest[8:12], rest[12:]
    for o, rider in zip(outs, riders):
        o[pl.ds(128, 64), :] = rider[...]
    put_pieces(pieces, at[Y], a)

    def put(ref, count, first, half):
        part = dot_rows(ref[...].reshape(count * 64, 512), a[...])
        for i in range(count):
            y[rows_of(128 * (first + i) + 64 * half, 64), :] = part[64 * i : 64 * i + 64]

    put(t_own, 4, 0, at[XL])
    put(t_one, 2, 2 * at[C], 1 - at[XL])
    put(t_two, 2, 2 * (1 - at[C]), 1 - at[XL])
    put_parts(y, at[Z], outs)


def cross_even_kernel(at, x_own, x_sib, a_own, *rest):
    o0, o1, o2, o3, a, y = rest[-6:]
    for r in range(4):
        row = 128 * (at[X] ^ at[Y] ^ r)
        theirs = rest[0][r, pl.ds(128, 64), :] if len(rest) > 6 else x_sib[pl.ds(512 + 64 * r, 64), :]
        a[rows_of(row + 64 * at[C], 64), :] = a_own[r]
        a[rows_of(row + 64 * (1 - at[C]), 64), :] = theirs
    cross_of(at, x_own, x_sib, a, y, (o0, o1, o2, o3))


def cross_odd_kernel(at, x_own, x_sib, a0, a1, a2, a3, o0, o1, o2, o3, a, y):
    for r, piece in enumerate((a0, a1, a2, a3)):
        a[rows_of(128 * (at[X] ^ at[Y] ^ r), 128), :] = piece[pl.ds(128, 128), :]
    cross_of(at, x_own, x_sib, a, y, (o0, o1, o2, o3))


def cross_of(at, x_own, x_sib, a, y, outs):
    for ref, half in ((x_own, at[C]), (x_sib, 1 - at[C])):
        y[rows_of(256 * half, 256), :] = dot_cols(ref[pl.ds(0, 512), :], a[...])
    put_parts(y, at[Z], outs)


def close_odd_kernel(at, b0, b1, b2, b3, b_sib, y0, y1, y2, y3, *rest):
    outs, (b, x, y) = rest[:4], rest[4:]
    put_pieces((y0, y1, y2, y3), at[Z], y)
    for r, own in enumerate((b0, b1, b2, b3)):
        rows = rows_of(128 * (at[X] ^ r), 128)
        b[rows, rows_of(256 * at[C], 256)] = own[pl.ds(0, 128), :]
        b[rows, rows_of(256 * (1 - at[C]), 256)] = b_sib[r, pl.ds(0, 128), :]
    x[...] = dot_cols(b[...], y[...])
    put_parts(x, at[Y], outs)


def close_even_kernel(slot, at, b0, b1, b2, b3, b_sib, y0, y1, y2, y3, *rest):
    outs, (b, x, y) = rest[:4], rest[4:]
    put_pieces((y0, y1, y2, y3), at[Z], y)
    here = pl.ds(128 * slot, 128)
    for r, own in enumerate((b0, b1, b2, b3)):
        cols = rows_of(128 * (at[Y] ^ r), 128)
        for k in range(4):
            b[rows_of(128 * k + 64 * at[C], 64), cols] = own[pl.ds(64 * k, 64), here]
            b[rows_of(128 * k + 64 * (1 - at[C]), 64), cols] = b_sib[r, pl.ds(64 * k, 64), here]
    x[...] = dot_cols(b[...], y[...])
    put_parts(x, at[X], outs)


def pair_kernel(at, mask, d0, d1, d2, d3, factor, local, keep, give):
    low, high = pl.ds(0, 256), pl.ds(256, 256)
    dealt = (d0, d1, d2, d3)

    def factors(ref):
        for r, d in enumerate(dealt):
            ref[at[LANE] ^ r, 0] = d[0, :, low]
            ref[at[LANE] ^ r, 1] = d[0, :, high]

    def nothing(ref, slots):
        for s in range(4):
            for k in slots:
                ref[s, k] = jnp.zeros((64, 256), jnp.float32)

    @pl.when(at[C] == 0)
    def _():
        for r, d in enumerate(dealt):
            keep[at[LANE] ^ r, 2] = d[1, :, low]
            give[at[LANE] ^ r, 2] = d[1, :, high]
        for ref in (keep, give):
            nothing(ref, (3, 4))

        @pl.when(at[XL] == 0)
        def _():
            factors(keep)
            nothing(give, (0, 1))

        @pl.when(at[XL] == 1)
        def _():
            factors(give)
            nothing(keep, (0, 1))

    @pl.when(at[C] == 1)
    def _():
        for r, d in enumerate(dealt):
            s = at[LANE] ^ r
            keep[s, 1] = d[0, :, high]
            give[s, 1] = d[0, :, low]
            for h, cols in enumerate((low, high)):
                keep[s, 3 + h] = d[1, :, cols]
                give[s, 3 + h] = d[1, :, cols]
        for s in range(4):
            for k, ref in ((0, factor), (2, local)):
                for i in range(2):
                    here = pl.ds(128 * i, 128)
                    give[s, k, :, here] = ref[:, pl.ds(512 * i + 128 * s, 128)]
                    keep[s, k, :, here] = ref[:, pl.ds(512 * (i + 2) + 128 * s, 128)]


def row_kernel(at, keep, got, *outs):
    rows, locals_, t_all = outs[:4], outs[4:8], outs[8]

    def fill(odd, even):
        for r, (a, e) in enumerate(zip(rows, locals_)):
            s = at[X] ^ r
            for k in range(2):
                a[k] = odd[s, k]
                a[2 + k] = even[s, k]
            e[0] = odd[s, 2]
            e[1] = even[s, 2]
        for s in range(4):
            for h in range(2):
                t_all[s, :, pl.ds(256 * h, 256)] = odd[s, 3 + h]
        for i, a in enumerate((rows[1], rows[3])):
            for h in range(2):
                a[4 + h] = odd[2 * at[C] + i, 3 + h]

    @pl.when(at[C] == 0)
    def _():
        fill(got, keep)

    @pl.when(at[C] == 1)
    def _():
        fill(keep, got)


def base_kernel(at, a0, a1, a2, a3, *outs):
    uppers, mixed, riders, t_one = outs[0], outs[1:3], outs[3:7], outs[7]
    for r, a in enumerate((a0, a1, a2, a3)):
        s = at[X] ^ r
        n = s // 2
        rows = rows_of(64 * lax.rem(s, 2), 64)
        for i in range(2):

            @pl.when(n == i)
            def _():
                uppers[rows_of(128 * (1 - i) + 64 * lax.rem(s, 2), 64), :] = a[0]
                mixed[i][rows, :] = a[1]

            @pl.when((n == i) & (lax.rem(s, 2) == at[C]))
            def _():
                for h in range(2):
                    mixed[i][pl.ds(128 + 64 * h, 64), :] = a[2 + h]

        @pl.when(lax.rem(s, 2) == at[C])
        def _():
            for k, rider in enumerate(riders):
                v = at[Z] ^ k
                block = a[2 + v // 2, :, rows_of(128 * lax.rem(v, 2), 128)]
                rider[:, rows_of(128 * n, 128)] = block

    for i, a in enumerate((a1, a3)):
        for h in range(2):
            t_one[i, :, pl.ds(256 * h, 256)] = a[4 + h]


def share_kernel(at, a0, a1, a2, a3, give, a_own):
    for r, a in enumerate((a0, a1, a2, a3)):
        give[r, pl.ds(0, 128), :] = a[pl.ds(0, 128), :]
        give[r, pl.ds(128, 64), :] = a[rows_of(128 + 64 * (1 - at[C]), 64), :]
        a_own[r] = a[rows_of(128 + 64 * at[C], 64), :]


def column_kernel(at, e0, e1, e2, e3, out):
    for r, e in enumerate((e0, e1, e2, e3)):
        out[rows_of(64 * (at[Z] ^ r), 64), :] = e[pl.ds(128, 64), :]


def local_kernel(at, e0, e1, e2, e3, m0, m1, m2, m3, *outs):
    a_own, a_give = outs[4:]
    for r, m in enumerate((m0, m1, m2, m3)):
        a_own[r] = m[rows_of(128 + 64 * at[C], 64), :]
        a_give[pl.ds(64 * r, 64), :] = m[rows_of(128 + 64 * (1 - at[C]), 64), :]
    for r, e in enumerate((e0, e1, e2, e3)):
        s = at[X] ^ r
        for n in range(2):

            @pl.when(s // 2 == n)
            def _():
                rows = rows_of(64 * lax.rem(s, 2), 64)
                outs[2 * n][rows, :] = e[1]
                outs[2 * n + 1][rows, :] = e[0]


def early_kernel(at, x1, y1, x2, y2, x3, y3, *outs):
    for r, out in enumerate(outs):
        for s in range(4):

            @pl.when((at[X] ^ r) == s)
            def _():
                rows = pl.ds(64 * (s % 2), 64)
                steps = ((x2, y2), (x3, y3)) if s // 2 else ((x1, y1), (x1, y1))
                for n, step in enumerate(steps):
                    for k, ref in enumerate(step):
                        out[n, k] = ref[rows, :]


def late_kernel(at, x0, y0, *outs):
    for r, out in enumerate(outs):
        rows = rows_of(64 * lax.rem(at[X] ^ r, 2), 64)
        out[0] = x0[rows, :]
        out[1] = y0[rows, :]


def meet_kernel(at, e0, e1, e2, e3, l0, l1, l2, l3, *outs):
    rest = outs[4]
    for k, (early, late) in enumerate(((e0, l0), (e1, l1), (e2, l2), (e3, l3))):
        rest[at[X] ^ k] = early[1]
        for r in range(4):
            here = (at[X] ^ at[Y] ^ k) == r

            @pl.when(here & (at[X] // 2 == 0))
            def _():
                outs[r][...] = late[...]

            @pl.when(here & (at[X] // 2 == 1))
            def _():
                outs[r][...] = early[0]


def turn_kernel(at, h0, h1, h2, h3, rest, keep, give):
    @pl.when(at[C] == 0)
    def _():
        for r, h in enumerate((h0, h1, h2, h3)):
            keep[at[Y] ^ r] = h[...]
        give[...] = rest[...]

    @pl.when(at[C] == 1)
    def _():
        for r, h in enumerate((h0, h1, h2, h3)):
            give[at[Y] ^ r] = h[...]
        keep[...] = rest[...]


def finish_kernel(at, mask, keep, got, diag, off):
    for ref, half in ((keep, at[C]), (got, 1 - at[C])):
        for s in range(4):
            for i in range(2):
                block = 4 * (2 * half + i) + s
                cols = rows_of(128 * block, 128)
                kept = mask[block]
                diag[:, cols] = ref[s, 0, :, pl.ds(128 * i, 128)] * kept
                off[:, cols] = -ref[s, 1, :, pl.ds(128 * i, 128)] * kept


def local(kernel, at, args, shapes, scratch=(), copies=0, scalars=(), far=(), flops=0, out_far=0):
    vmem = pl.BlockSpec(memory_space=pltpu.VMEM)
    smem = pl.BlockSpec(memory_space=pltpu.SMEM)
    hbm = pl.BlockSpec(memory_space=pltpu.HBM)
    moved = sum(int(np.prod(a.shape)) for a in args) + sum(int(np.prod(s)) for s in shapes)
    scratch = [pltpu.VMEM(s, jnp.float32) for s in scratch]
    if copies:
        scratch.append(pltpu.SemaphoreType.DMA((copies,)))
    return pl.pallas_call(
        kernel,
        out_shape=[jax.ShapeDtypeStruct(s, jnp.float32) for s in shapes],
        in_specs=[smem] * (1 + len(scalars)) + [hbm] * len(far) + [vmem] * len(args),
        out_specs=[vmem] * (len(shapes) - out_far) + [hbm] * out_far,
        scratch_shapes=scratch,
        compiler_params=pltpu.CompilerParams(vmem_limit_bytes=16 * 1024 * 1024),
        cost_estimate=pl.CostEstimate(flops=0, bytes_accessed=1024, transcendentals=0),
    )(at, *scalars, *far, *args)


def product(kernel, at, args, scratch, rows=128, far=(), copies=0):
    work = 6 * 512 * 512 * 256
    return local(
        kernel, at, args, [(rows, 256)] * 4, scratch, copies=copies, far=far, flops=work
    )


def on_device(inv_local, coupling, tail_block, adjacency):
    xh, co, z, y, xl = (lax.axis_index(a) for a in AXES)
    x = 2 * xh + xl
    at = jnp.stack([x, y, z, co, xl, jnp.where(co == 0, y, z)]).astype(jnp.int32)
    along = {axis: functools.partial(partner, axis) for axis in "xyz"}
    piece, half_piece = (128, 256), (64, 256)
    wide, square = (512, 256), (512, 512)
    x8, y8 = ("xh", "xl", "co"), ("y", "co")

    factor, own, tail = coupling[0], inv_local[0], tail_block
    lane = jnp.where(co == 0, y, z)

    def dealt_for(r):
        def columns(a):
            v = lane ^ r
            starts = [jnp.where(co == 0, 512 * k + 128 * v, 512 * v + 128 * k) for k in range(4)]
            return jnp.concatenate([lax.dynamic_slice(a, (0, s), (64, 128)) for s in starts], axis=1)

        return jnp.stack([columns(factor), jnp.where(co == 0, columns(own), columns(tail))])

    count = adjacency.shape[0]
    joined = jnp.maximum(adjacency, jnp.eye(count, dtype=jnp.int32)).astype(jnp.float32)
    mask = lax.dynamic_index_in_dim(joined, (z * 8 + y * 2 + xl) * 64 // TILE, 0, keepdims=False)
    dealt = exchanged([dealt_for(r) for r in range(4)], deal)
    keep, give = local(
        pair_kernel, at, dealt + [factor, own], [(4, 5, 64, 256)] * 2, scalars=[mask]
    )
    got = send(give, to_other_core)
    *rows, t_all = local(
        row_kernel,
        at,
        [keep, got],
        [(n, 64, 256) for n in (4, 6, 4, 6)] + [(2, 64, 256)] * 4 + [(4, 64, 512)],
    )
    rows, rows_local = rows[:4], rows[4:]
    (uppers, mixed, lowers, *riders, t_one) = local(
        base_kernel,
        at,
        exchanged(rows, along["x"]),
        [(256, 256)] * 3 + [half_piece] * 4 + [(2, 64, 512)],
    )
    pieces = gathered(uppers, "y")
    lowers = gathered(lowers, "x")
    (t_aside,) = after([t_one], pieces[1])
    t_two = send(t_aside, to_other_core)
    pieces = list(after(pieces, tuple(lowers)))
    parts = product(
        cross_tail_kernel, at, [t_all, t_one, t_two] + pieces + riders, [wide, wide], 192
    )
    b_sib = send(jnp.stack([a[:128] for a in lowers]), to_other_core)
    rows_local = after(rows_local, parts[0])
    cross, columns = scattered(parts, "z")
    rows_local = exchanged(rows_local, along["x"])
    crosses, blocks = {3: cross}, {}
    (on_y,) = local(column_kernel, at, columns, [(256, 256)])

    for t in (3, 2, 1, 0):
        odd = t % 2 == 1
        first, second = ("y", "x") if odd else ("x", "y")
        if t == 0:
            early = [a[s] for s in (1, 2, 3) for a in (blocks, crosses)]
            early = local(early_kernel, at, early, [(2, 2, 64, 256)] * 4)
            early = exchanged(early, along["x"])
        if t < 3:
            mine = gathered(blocks[t + 1], second)
            if t == 2:
                (mixed,) = after([mixed], blocks[3])
                mixed = gathered(mixed, "x")
                x_own = jnp.concatenate(after(mine + [a_give], tuple(mixed)))
                (on_y,) = after([on_y], x_own)
                on_y = gathered(on_y, "y")
            else:
                x_own = jnp.concatenate(mine)
            args = [x_own, send(x_own, to_other_core)]
            if odd:
                args += pieces
            else:
                args += [a_own] if t else [a_own, b_sib]
            kernel = cross_odd_kernel if odd else cross_even_kernel
            parts = product(kernel, at, args, [wide, wide])
            cross, _ = scattered(parts, "z")
            crosses[t] = cross
        whole = gathered(cross, "z")
        if t == 0:
            whole = list(after(whole, tuple(early)))
        if t == 2:
            on_y = list(after(on_y, whole[2]))
            on_y_sib = send(jnp.stack(on_y), to_other_core)
        args = list(lowers) + [b_sib] if odd else on_y + [on_y_sib]
        kernel = close_odd_kernel if odd else functools.partial(close_even_kernel, t // 2)
        args += whole
        parts = product(kernel, at, args, [square, wide, wide])
        if t == 3:
            rows_local = after(rows_local, parts[0])
            *locals_, a_own, a_give = local(
                local_kernel, at, list(rows_local) + lowers, [piece] * 4 + [(4, *half_piece), (256, 256)]
            )
        if t == 2:
            lowers = list(after(mixed, parts[0]))
            give, a_own = local(share_kernel, at, lowers, [(4, 192, 256), (4, *half_piece)])
            b_sib = send(give, to_other_core)
        blocks[t] = scattered(parts, first)[0] + locals_[t]

    late = local(late_kernel, at, [blocks[0], crosses[0]], [(2, 64, 256)] * 4)
    late = [late[0]] + [
        send(late[r], along["x"](r), lambda x, **_: (x ^ r) // 2 == 0) for r in (1, 2, 3)
    ]
    *turned, rest = local(
        meet_kernel, at, early + late, [(2, 64, 256)] * 4 + [(4, 2, 64, 256)]
    )
    turned = exchanged(turned, along["y"])
    keep, give = local(turn_kernel, at, turned + [rest], [(4, 2, 64, 256)] * 2)
    got = send(give, to_other_core)
    diag, off = local(finish_kernel, at, [keep, got], [(64, 2048)] * 2, scalars=[mask])
    return diag[None], off[None]


def solution(mesh):
    fine = Mesh(mesh.devices.reshape(SIZES), AXES)
    rows = P(("xh", "co"), ("z", "y", "xl"), None)
    return jax.shard_map(
        on_device,
        mesh=fine,
        in_specs=(rows, rows, P(("z", "y", "xl"), None), P()),
        out_specs=(rows, rows),
        check_vma=False,
    )
```
